256 devices in a mesh: band: 64 (over z, y, core), chan: 4 (over x).
Axes of the slice: x: 4, y: 4, z: 8, core: 2. Of those that a mesh axis runs over, the one named last changes fastest.
Arguments:
- grid_in: bfloat16 [524288, 474], P('band'), may hold values from -6 to 6
- w_embed: bfloat16 [474, 512], P(None, 'chan'), may hold values from -0.25 to 0.25
- send_order: int32 [64, 64], P('band'), may hold values from 0 to 63, each once within a row
- enc_coef: bfloat16 [6144, 128, 128], P('band'), may hold values from -0.125 to 0.125
- enc_slot: int32 [64, 96], P('band'), may hold values from 0 to 63
- enc_dest: int32 [64, 96], P('band'), may hold values from 0 to 4
- mesh_in: bfloat16 [40960, 512], P('band', 'chan'), may hold values from -6 to 6
- proc_coef: bfloat16 [3072, 128, 128], P('band'), may hold values from -0.15625 to 0.15625
- proc_src: int32 [64, 48], P('band'), may hold values from 0 to 14
- proc_dest: int32 [64, 48], P('band'), may hold values from 0 to 4
- w_node: bfloat16 [512, 512], P(None, 'chan'), may hold values from -0.25 to 0.25
- out_grad: bfloat16 [40960, 512], P('band', 'chan'), may hold values from -6 to 6
Outputs:
- mesh_out: bfloat16 [40960, 512], P('band', 'chan')
- mesh_grad: float32 [40960, 512], P('band', 'chan')
- grad_embed: float32 [474, 512], P(None, 'chan')
- grad_node: float32 [512, 512], P(None, 'chan')
The draws below stay inside these ranges and needn't reach their ends.
All inputs are finite; a program needn't handle non-finite values.
Results may differ from the reference program's by a relative error of at most 0.006.
Values may be sent and summed in bfloat16 or wider, within the bound.
A program may use at most 128 MiB of HBM per device.

```python
import jax
import jax.numpy as jnp
from jax import lax

C_IN = 474
LAT = 512
BLK = 128
CAP = 1
MB_DEV = 5
ENC_PAIRS = 96
PROC_PAIRS = 48
GB_DEV = 64
GRID = 524288
MESH = 40960
N_BAND = 64


def set_ends(result, stream_key, low, largest):
    longest = result.shape.index(max(result.shape))
    spots = []
    for shift in (0, 1):
        where = [jax.random.randint(jax.random.fold_in(stream_key, axis), (), 0, length) for axis, length in enumerate(result.shape)]
        where[longest] = (where[longest] + shift) % result.shape[longest]
        spots.append(tuple(where))
    return result.at[spots[0]].set(low).at[spots[1]].set(largest)


def steps_of(stream_key, shape, cuts, low, high):
    factor_of = 1.0
    for position, blocks in cuts:
        draws = jax.random.uniform(jax.random.fold_in(jax.random.fold_in(stream_key, 6), position), (blocks,), jnp.float32, low / len(cuts), high / len(cuts))
        factor_of = factor_of * jnp.repeat(jnp.exp(draws), shape[position] // blocks).reshape((-1,) + (1,) * (len(shape) - 1 - position))
    return factor_of


def noise(own_key, dims, deviation, limit, split=(), kind=jnp.bfloat16):
    gain = steps_of(own_key, dims, split, -0.22, 0.18) if split else 1.0
    drawn = jax.random.normal(own_key, dims, jnp.float32) * deviation * gain
    return jnp.minimum(jnp.maximum(drawn, -limit), limit).astype(kind)


def setup_inputs(seed: int = 0) -> dict:
    keys = jax.random.split(jax.random.key(seed), 13)
    return {
        "grid_in": noise(keys[0], (GRID, C_IN), 1.0, 6.0, ((0, 64),)),
        "w_embed": noise(keys[1], (C_IN, LAT), C_IN ** -0.5, 0.25, ((1, 4),)),
        "send_order": jax.vmap(lambda own: jax.random.permutation(own, GB_DEV))(jax.random.split(keys[2], N_BAND)).reshape((N_BAND, GB_DEV)).astype(jnp.int32),
        "enc_coef": noise(keys[3], (N_BAND * ENC_PAIRS, BLK, BLK), (BLK * ENC_PAIRS // MB_DEV) ** -0.5, 0.125, ((0, 64),)),
        "enc_slot": set_ends(jax.random.randint(keys[4], (N_BAND, ENC_PAIRS), 0, GB_DEV), jax.random.fold_in(keys[4], 1), 0, GB_DEV - 1).astype(jnp.int32),
        "enc_dest": set_ends(jax.random.randint(keys[5], (N_BAND, ENC_PAIRS), 0, MB_DEV), jax.random.fold_in(keys[5], 1), 0, MB_DEV - 1).astype(jnp.int32),
        "mesh_in": noise(keys[6], (MESH, LAT), 1.0, 6.0, ((0, 64), (1, 4))),
        "proc_coef": noise(keys[7], (N_BAND * PROC_PAIRS, BLK, BLK), (BLK * PROC_PAIRS // MB_DEV) ** -0.5, 0.15625, ((0, 64),)),
        "proc_src": set_ends(jax.random.randint(keys[8], (N_BAND, PROC_PAIRS), 0, 3 * MB_DEV), jax.random.fold_in(keys[8], 1), 0, (3 * MB_DEV) - 1).astype(jnp.int32),
        "proc_dest": set_ends(jax.random.randint(keys[9], (N_BAND, PROC_PAIRS), 0, MB_DEV), jax.random.fold_in(keys[9], 1), 0, MB_DEV - 1).astype(jnp.int32),
        "w_node": noise(keys[10], (LAT, LAT), LAT ** -0.5, 0.25, ((1, 4),)),
        "out_grad": noise(keys[11], (MESH, LAT), 1.0, 6.0, ((0, 64), (1, 4))),
    }


def silu_slope(values):
    sigma = jax.nn.sigmoid(values)
    return sigma * (1.0 + values * (1.0 - sigma))


def select_matrix(targets, count):
    return (targets[None, :] == jnp.arange(count, dtype=jnp.int32)[:, None]).astype(jnp.float32)


def collect(weights, source, source_ids, dest_ids, count):
    picked = source[source_ids].astype(jnp.float32)
    messages = jnp.einsum('pij,pjc->pic', weights.astype(jnp.float32), picked)
    return jnp.einsum('bp,pic->bic', select_matrix(dest_ids, count), messages, precision=lax.Precision.HIGHEST)


def spread(weights, target, source_ids, dest_ids, count):
    picked = target[dest_ids].astype(jnp.float32)
    messages = jnp.einsum('pji,pjc->pic', weights.astype(jnp.float32), picked)
    return jnp.einsum('sp,pic->sic', select_matrix(source_ids, count), messages, precision=lax.Precision.HIGHEST)


def reference(grid_in, w_embed, send_order, enc_coef, enc_slot, enc_dest, mesh_in, proc_coef, proc_src, proc_dest, w_node, out_grad):
    rows_in = grid_in.reshape(N_BAND, GB_DEV * BLK, C_IN)

    def embed(band_rows):
        pre_grid = jnp.dot(band_rows, w_embed, preferred_element_type=jnp.float32)
        return jax.nn.silu(pre_grid).astype(jnp.bfloat16).reshape(GB_DEV, BLK, LAT)

    latent = lax.map(embed, rows_in)
    sent = jax.vmap(lambda blocks, order_row: blocks[order_row])(latent, send_order)
    received = sent.reshape(N_BAND, N_BAND, CAP, BLK, LAT).transpose(1, 0, 2, 3, 4).reshape(N_BAND, GB_DEV, BLK, LAT)
    enc_weights = enc_coef.reshape(N_BAND, ENC_PAIRS, BLK, BLK)
    enc_pre = lax.map(lambda inputs: collect(inputs[0], inputs[1], inputs[2], inputs[3], MB_DEV),
                      (enc_weights, received, enc_slot, enc_dest)).reshape(MESH, LAT)
    mesh_one = (mesh_in.astype(jnp.float32) + jax.nn.silu(enc_pre)).astype(jnp.bfloat16)
    blocks = mesh_one.reshape(N_BAND, MB_DEV, BLK, LAT)
    zeros_pad = jnp.zeros((1, MB_DEV, BLK, LAT), jnp.bfloat16)
    lower_rim = jnp.concatenate([zeros_pad, blocks[:-1]], axis=0)
    upper_rim = jnp.concatenate([blocks[1:], zeros_pad], axis=0)
    extended = jnp.concatenate([lower_rim, blocks, upper_rim], axis=1)
    proc_weights = proc_coef.reshape(N_BAND, PROC_PAIRS, BLK, BLK)
    proc_pre = lax.map(lambda inputs: collect(inputs[0], inputs[1], inputs[2], inputs[3], MB_DEV),
                       (proc_weights, extended, proc_src, proc_dest)).reshape(MESH, LAT)
    hidden = jax.nn.silu(proc_pre).astype(jnp.bfloat16)
    mesh_out = (mesh_one.astype(jnp.float32) + jnp.dot(hidden, w_node, preferred_element_type=jnp.float32)).astype(jnp.bfloat16)
    grad_node = jnp.dot(hidden.T, out_grad, preferred_element_type=jnp.float32)
    grad_hidden = jnp.dot(out_grad, w_node.T, preferred_element_type=jnp.float32)
    grad_proc = (grad_hidden * silu_slope(proc_pre)).astype(jnp.bfloat16).reshape(N_BAND, MB_DEV, BLK, LAT)
    grad_extended = lax.map(lambda inputs: spread(inputs[0], inputs[1], inputs[2], inputs[3], 3 * MB_DEV),
                            (proc_weights, grad_proc, proc_src, proc_dest))
    zeros_grad = jnp.zeros((1, MB_DEV, BLK, LAT), jnp.float32)
    from_upper = jnp.concatenate([grad_extended[1:, :MB_DEV], zeros_grad], axis=0)
    from_lower = jnp.concatenate([zeros_grad, grad_extended[:-1, 2 * MB_DEV:]], axis=0)
    mesh_grad = out_grad.astype(jnp.float32).reshape(N_BAND, MB_DEV, BLK, LAT) + grad_extended[:, MB_DEV:2 * MB_DEV] + from_upper + from_lower
    mesh_grad = mesh_grad.reshape(MESH, LAT)
    grad_enc = (mesh_grad * silu_slope(enc_pre)).astype(jnp.bfloat16).reshape(N_BAND, MB_DEV, BLK, LAT)
    grad_received = lax.map(lambda inputs: spread(inputs[0], inputs[1], inputs[2], inputs[3], GB_DEV),
                            (enc_weights, grad_enc, enc_slot, enc_dest))
    grad_sent = grad_received.reshape(N_BAND, N_BAND, CAP, BLK, LAT).transpose(1, 0, 2, 3, 4).reshape(N_BAND, GB_DEV, BLK, LAT)
    grad_grid = jax.vmap(lambda values, order_row: jnp.zeros_like(values).at[order_row].set(values))(grad_sent, send_order)

    def embed_back(inputs):
        band_rows, band_grad = inputs
        pre_grid = jnp.dot(band_rows, w_embed, preferred_element_type=jnp.float32)
        grad_pre = (band_grad.reshape(GB_DEV * BLK, LAT) * silu_slope(pre_grid)).astype(jnp.bfloat16)
        return jnp.dot(band_rows.T, grad_pre, preferred_element_type=jnp.float32)

    grad_embed = jnp.sum(lax.map(embed_back, (rows_in, grad_grid)), axis=0)
    return mesh_out, mesh_grad, grad_embed, grad_node
```

```python
import jax
import jax.numpy as jnp
from jax import lax
from jax.experimental import pallas as pl
from jax.experimental.pallas import tpu as pltpu
from jax.sharding import PartitionSpec as P

MESH = pl.DeviceIdType.MESH
F32 = jnp.float32
BF = jnp.bfloat16
NB = 64
NX = 4
C_IN = 474
CP = 480
LAT = 512
W = 128
T = NB // NX
EP = 96
PP = 48
MB = 5
MR = MB * W
ER = T * W
NT = 32
CELLS = MB * T


def dot(a, b):
    return jnp.dot(a, b, preferred_element_type=F32)


def slope_of(v, s):
    return s * (1.0 + v * (1.0 - s))


def al(v, m):
    return pl.multiple_of(v, m)


def kernel(
    order, eslot, edest, psrc, pdest, grid, wemb, ecoef, meshin, pcoef, wnode, ograd,
    mesh_out, mesh_grad, gemb, gnode,
    gv, stage, recv, we_all, wtmp, og_all, wn, wr_all, mi, ce, cp,
    wide, cells, a_enc, a_proc, at_proc, gh, slope,
    part, enc_sum, enc_slope_f, rs1, ext, hid_all, hb_out, hb_in, mid, gn_out, gn_in, ge_all, gp,
    gemb_f, gemb_out, rs2, red, ra, sb, rb, fin, fin2,
    lsem, g_s, a_s, a_r, x_s, x_r, h_s, h_r, b_s, b_r, c_s, c_r, t_s, t_r, u_s, u_r,
):
    me = lax.axis_index("band")
    x = lax.axis_index("chan")
    core = lax.rem(me, 2)
    chip = lax.div(me, 2)
    mine = pl.ds(al(x * W, W), W)

    def to_band(src, dst, ss, rs, band):
        return pltpu.make_async_remote_copy(src, dst, ss, rs, device_id={"band": band}, device_id_type=MESH)

    def to_chan(src, dst, ss, rs, chan):
        return pltpu.make_async_remote_copy(src, dst, ss, rs, device_id={"chan": chan}, device_id_type=MESH)

    def peer(dx):
        return lax.rem(x + dx, NX)

    def cols(c):
        return pl.ds(al(c * W, W), W)

    def rows_of(c):
        return pl.ds(al(c * W, W), W)

    def load_block(b):
        return pltpu.make_async_copy(grid.at[:, cols(b)], gv.at[b], g_s.at[b])

    def load_start(b, _):
        load_block(b).start()
        return 0

    lax.fori_loop(0, NB, load_start, 0)
    load_wemb = pltpu.make_async_copy(wemb, wtmp, lsem.at[1])
    load_og = pltpu.make_async_copy(ograd, og_all.at[:, mine], lsem.at[2])
    load_wn = pltpu.make_async_copy(wnode, wn, lsem.at[3])
    load_mi = pltpu.make_async_copy(meshin, mi, lsem.at[4])
    load_ce = pltpu.make_async_copy(ecoef, ce, lsem.at[5])
    load_cp = pltpu.make_async_copy(pcoef, cp, lsem.at[6])
    load_wemb.start()
    load_og.start()
    load_wn.start()

    barrier = pltpu.get_barrier_semaphore()

    def greet(j, _):
        pl.semaphore_signal(barrier, inc=1, device_id={"band": lax.rem(me + j, NB)}, device_id_type=MESH)
        return 0

    lax.fori_loop(1, NB, greet, 0)
    for dx in range(1, NX):
        pl.semaphore_signal(barrier, inc=1, device_id={"chan": peer(dx)}, device_id_type=MESH)

    stage[:, CP - 16 :, :] = jnp.zeros((T, 16, W), BF)

    def load_wait(b, _):
        load_block(b).wait()
        return 0

    lax.fori_loop(0, NB, load_wait, 0)
    pl.semaphore_wait(barrier, NB - 1 + NX - 1)

    def grid_copy(t):
        d = lax.rem(me + x + NX * t, NB)
        return to_band(stage.at[t], recv.at[:, cols(t)], a_s.at[t], a_r.at[t], d)

    def send_grid(t, _):
        d = lax.rem(me + x + NX * t, NB)
        stage[t, :C_IN, :] = gv[order[0, d]]

        @pl.when(x + t != 0)
        def _():
            grid_copy(t).start()

        return 0

    lax.fori_loop(0, T, send_grid, 0)
    load_mi.start()
    load_ce.start()
    load_cp.start()

    @pl.when(x == 0)
    def _():
        recv[:, 0:W] = stage[0]

    load_wemb.wait()
    we_all[mine, CP - W : CP] = jnp.zeros((W, W), BF)
    we_all[mine, :C_IN] = wtmp[...].astype(F32).T.astype(BF)
    load_og.wait()
    load_wn.wait()
    wr_all[:, mine] = wn[mine, :]

    def early(dx):
        p = peer(dx)
        return (
            to_chan(we_all.at[mine, :], we_all.at[mine, :], x_s.at[0, dx], x_r.at[0, dx], p),
            to_chan(og_all.at[:, mine], og_all.at[:, mine], x_s.at[1, dx], x_r.at[1, dx], p),
            to_chan(wn.at[rows_of(p), :], wr_all.at[:, mine], x_s.at[2, dx], x_r.at[2, dx], p),
        )

    for dx in range(1, NX):
        for c in early(dx):
            c.start()

    def sum_cells(coef, pairs, hits):
        wide[0 : pairs * W, :] = coef[...].astype(F32)
        pick = jnp.where(hits, 1.0, 0.0).astype(BF)

        def one(i, _):
            line = wide[pl.ds(i, pairs, stride=W), :].astype(BF)
            cells[pl.ds(i, CELLS, stride=W), :] = dot(pick, line)
            return 0

        lax.fori_loop(0, W, one, 0, unroll=4)

    def cell_ids(pairs):
        cell = lax.broadcasted_iota(jnp.int32, (CELLS, pairs), 0)
        return lax.shift_right_logical(cell, 4), lax.bitwise_and(cell, T - 1)

    load_ce.wait()
    cell_m, cell_t = cell_ids(EP)
    cell_slot = lax.bitwise_and(me - x - NX * cell_t + 2 * NB, NB - 1)
    sum_cells(ce, EP, (edest[...] == cell_m) & (eslot[...] == cell_slot))

    def enc_cells(t, _):
        for m in range(MB):
            a_enc[m * W : (m + 1) * W, cols(t)] = cells[rows_of(m * T + t), :].astype(BF)
        return 0

    lax.fori_loop(0, T, enc_cells, 0)

    load_cp.wait()
    cell_m, cell_s = cell_ids(PP)
    sum_cells(cp, PP, (pdest[...] == cell_m) & (psrc[...] == cell_s))

    def proc_cells(s, _):
        for m in range(MB):
            block = cells[rows_of(m * T + s), :]
            a_proc[m * W : (m + 1) * W, cols(s)] = block.astype(BF)
            at_proc[rows_of(s), m * W : (m + 1) * W] = block.T.astype(BF)
        return 0

    lax.fori_loop(0, 3 * MB, proc_cells, 0)

    for dx in range(1, NX):
        for c in early(dx):
            c.wait_recv()
    gh[...] = lax.dot_general(og_all[...], wr_all[...], (((1,), (1,)), ((), ())), preferred_element_type=F32)

    def dot_nt(a, b):
        return lax.dot_general(a, b, (((1,), (1,)), ((), ())), preferred_element_type=F32)

    enc_sum[...] = jnp.zeros((MR, LAT), F32)

    def embed(u, _):
        for v in range(2):
            t = 2 * u + v

            @pl.when(x + t != 0)
            def _():
                grid_copy(t).wait_recv()

        here = pl.ds(al(u * 2 * W, 2 * W), 2 * W)
        pre = dot(we_all[...], recv[:, here])
        sig = jax.nn.sigmoid(pre)
        latent = (pre * sig).astype(BF)
        slope[:, here] = slope_of(pre, sig)
        enc_sum[...] += dot_nt(a_enc[:, here], latent)
        return 0

    lax.fori_loop(0, T // 2, embed, 0)

    half = lax.div(x, 2)
    away = 1 - half
    twin = x + 1 - 2 * lax.rem(x, 2)
    far = (2 * away, 2 * away + 1)

    def two(h):
        return pl.ds(al(h * 2 * W, 2 * W), 2 * W)

    def enc_copy(c):
        return to_chan(part.at[:, cols(c)], rs1.at[x], c_s.at[0, c], c_r.at[0, x], c)

    part[:, two(away)] = enc_sum[:, two(away)].astype(BF)
    for c in far:
        enc_copy(c).start()
    part[:, cols(twin)] = enc_sum[:, cols(twin)].astype(BF)
    enc_copy(twin).start()

    load_mi.wait()
    enc_pre = enc_sum[:, mine]
    for dx in range(1, NX):
        p = peer(dx)
        to_chan(part.at[:, cols(p)], rs1.at[p], c_s.at[0, p], c_r.at[0, p], p).wait_recv()
        enc_pre = enc_pre + rs1[p].astype(F32)
    enc_sig = jax.nn.sigmoid(enc_pre)
    mesh_one = (mi[...].astype(F32) + enc_pre * enc_sig).astype(BF)
    enc_slope = slope_of(enc_pre, enc_sig)
    enc_slope_f[...] = enc_slope

    ext[MR : 2 * MR, :] = mesh_one
    has_low = me > 0
    has_high = me < NB - 1
    low = lax.rem(me + NB - 1, NB)
    high = lax.rem(me + 1, NB)
    own_ext = ext.at[MR : 2 * MR, :]
    halo_up = to_band(own_ext, ext.at[0:MR, :], h_s.at[0], h_r.at[0], high)
    halo_down = to_band(own_ext, ext.at[2 * MR : 3 * MR, :], h_s.at[1], h_r.at[1], low)
    pl.when(has_high)(halo_up.start)
    pl.when(has_low)(halo_down.start)
    mid[...] = dot(a_proc[:, MR : 2 * MR], mesh_one)

    @pl.when(me == 0)
    def _():
        ext[0:MR, :] = jnp.zeros((MR, W), BF)

    @pl.when(me == NB - 1)
    def _():
        ext[2 * MR : 3 * MR, :] = jnp.zeros((MR, W), BF)

    pl.when(has_low)(halo_up.wait_recv)
    pl.when(has_high)(halo_down.wait_recv)
    proc_pre = (
        mid[...]
        + dot(a_proc[:, 0:MR], ext[0:MR, :])
        + dot(a_proc[:, 2 * MR : 3 * MR], ext[2 * MR : 3 * MR, :])
    )
    proc_sig = jax.nn.sigmoid(proc_pre)
    hidden = (proc_pre * proc_sig).astype(BF)
    hid_all[:, mine] = hidden

    def hid_copy(c):
        return to_chan(hid_all.at[:, mine], hid_all.at[:, mine], c_s.at[1, c], c_r.at[1, x], c)

    for dx in range(1, NX):
        hid_copy(peer(dx)).start()
    grad_proc = (gh[...] * slope_of(proc_pre, proc_sig)).astype(BF)

    hb_out[0] = dot(at_proc[0:MR, :], grad_proc).astype(BF)
    back_down = to_band(hb_out.at[0], hb_in.at[0], b_s.at[0], b_r.at[0], low)
    pl.when(has_low)(back_down.start)
    hb_out[1] = dot(at_proc[2 * MR : 3 * MR, :], grad_proc).astype(BF)
    back_up = to_band(hb_out.at[1], hb_in.at[1], b_s.at[1], b_r.at[1], high)
    pl.when(has_high)(back_up.start)
    mid[...] = dot(at_proc[MR : 2 * MR, :], grad_proc) + og_all[:, mine].astype(F32)

    gn_out[...] = dot(hidden.astype(F32).T.astype(BF), og_all[...])
    gn_in[mine, :] = gn_out[:, mine]

    def gn_copy(c):
        return to_chan(gn_out.at[:, cols(c)], gn_in.at[mine, :], c_s.at[2, c], c_r.at[2, x], c)

    for dx in range(1, NX):
        gn_copy(peer(dx)).start()

    @pl.when(me == NB - 1)
    def _():
        hb_in[0] = jnp.zeros((MR, W), BF)

    @pl.when(me == 0)
    def _():
        hb_in[1] = jnp.zeros((MR, W), BF)

    pl.when(has_high)(back_down.wait_recv)
    pl.when(has_low)(back_up.wait_recv)
    total = mid[...] + hb_in[0].astype(F32) + hb_in[1].astype(F32)
    mesh_grad[...] = total
    ge_all[mine, :] = (total * enc_slope_f[...]).T.astype(BF)

    def ge_copy(c):
        return to_chan(ge_all.at[mine, :], ge_all.at[mine, :], c_s.at[3, c], c_r.at[3, x], c)

    def ge_wait(c):
        to_chan(ge_all.at[rows_of(c), :], ge_all.at[rows_of(c), :], c_s.at[3, c], c_r.at[3, c], c).wait_recv()

    for dx in range(1, NX):
        ge_copy(peer(dx)).start()

    for dx in range(1, NX):
        p = peer(dx)
        to_chan(hid_all.at[:, cols(p)], hid_all.at[:, cols(p)], c_s.at[1, p], c_r.at[1, p], p).wait_recv()
    mesh_out[...] = (ext[MR : 2 * MR, :].astype(F32) + dot(hid_all[...], wn[...])).astype(BF)

    def back(h):
        def piece(t, _):
            here = pl.ds(al(t * 512, 512), 512)
            msg = dot(ge_all[two(h), :], a_enc[:, here])
            gp[:, here] = (msg * slope[two(h), here]).astype(BF)
            return 0

        lax.fori_loop(0, ER // 512, piece, 0)
        gemb_f[...] = dot_nt(recv[...], gp[...])

    def ge2_copy(c):
        return to_chan(gemb_out.at[:, cols(c)], rs2.at[x], c_s.at[4, c], c_r.at[4, x], c)

    ge_wait(twin)
    back(half)
    red[0, 0:CP, :] = gemb_f[:, pl.ds(al(lax.rem(x, 2) * W, W), W)]
    red[0, CP:, :] = jnp.zeros((LAT - CP, W), F32)
    gemb_out[:, two(half)] = gemb_f[...].astype(BF)
    ge2_copy(twin).start()
    for c in far:
        ge_wait(c)
    back(away)
    gemb_out[:, two(away)] = gemb_f[...].astype(BF)
    for c in far:
        ge2_copy(c).start()

    for dx in range(1, NX):
        p = peer(dx)
        prow = pl.ds(al(p * W, W), W)
        to_chan(gn_out.at[:, cols(p)], gn_in.at[prow, :], c_s.at[2, p], c_r.at[2, p], p).wait_recv()
    red[1] = gn_in[...]
    for dx in range(1, NX):
        p = peer(dx)
        to_chan(gemb_out.at[:, cols(p)], rs2.at[p], c_s.at[4, p], c_r.at[4, p], p).wait_recv()
    red[0, 0:CP, :] += rs2[peer(1)].astype(F32) + rs2[peer(2)].astype(F32) + rs2[peer(3)].astype(F32)

    sibling = me + 1 - 2 * core
    keep = pl.ds(al(core * 256, 256), 256)
    give = pl.ds(al((1 - core) * 256, 256), 256)
    swap = to_band(red.at[:, give, :], ra, t_s.at[0], t_r.at[0], sibling)
    swap.start()
    swap.wait_recv()
    sb[...] = (red[:, keep, :] + ra[...]).astype(BF).reshape(NT, 16, W)

    def scatter_copy(j):
        d = lax.rem(chip + j, NT)
        return to_band(sb.at[d], rb.at[chip], u_s.at[0, j], u_r.at[0, j], 2 * d + core)

    def scatter(j, _):
        scatter_copy(j).start()
        return 0

    lax.fori_loop(1, NT, scatter, 0)
    rb[chip] = sb[chip]

    def scatter_wait(j, _):
        scatter_copy(j).wait_recv()
        return 0

    lax.fori_loop(1, NT, scatter_wait, 0)
    fin[chip] = jnp.sum(rb[...].astype(F32), axis=0).astype(BF)

    def gather_copy(j):
        d = lax.rem(chip + j, NT)
        return to_band(fin.at[chip], fin.at[chip], u_s.at[1, j], u_r.at[1, j], 2 * d + core)

    def gather(j, _):
        gather_copy(j).start()
        return 0

    lax.fori_loop(1, NT, gather, 0)

    def gather_wait(j, _):
        s = lax.rem(chip - j + NT, NT)
        to_band(fin.at[s], fin.at[s], u_s.at[1, j], u_r.at[1, j], 2 * s + core).wait_recv()
        return 0

    lax.fori_loop(1, NT, gather_wait, 0)
    swap_back = to_band(fin, fin2, t_s.at[1], t_r.at[1], sibling)
    swap_back.start()
    swap_back.wait_recv()
    own = fin[...].reshape(2, 256, W).astype(F32)
    other = fin2[...].reshape(2, 256, W).astype(F32)
    gnode[keep, :] = own[1]
    gnode[give, :] = other[1]

    @pl.when(core == 0)
    def _():
        gemb[0:256, :] = own[0]
        gemb[256:C_IN, :] = other[0][: C_IN - 256]

    @pl.when(core == 1)
    def _():
        gemb[0:256, :] = other[0]
        gemb[256:C_IN, :] = own[0][: C_IN - 256]

    def sent_grid(t, _):
        @pl.when(x + t != 0)
        def _():
            grid_copy(t).wait_send()

        return 0

    lax.fori_loop(0, T, sent_grid, 0)
    for dx in range(1, NX):
        p = peer(dx)
        for c in early(dx):
            c.wait_send()
        for f in (enc_copy, hid_copy, gn_copy, ge_copy, ge2_copy):
            f(p).wait_send()
    pl.when(has_high)(halo_up.wait_send)
    pl.when(has_low)(halo_down.wait_send)
    pl.when(has_low)(back_down.wait_send)
    pl.when(has_high)(back_up.wait_send)
    swap.wait_send()
    swap_back.wait_send()

    def sent_small(j, _):
        scatter_copy(j).wait_send()
        gather_copy(j).wait_send()
        return 0

    lax.fori_loop(1, NT, sent_small, 0)


def on_device(
    grid_in, w_embed, send_order, enc_coef, enc_slot, enc_dest, mesh_in, proc_coef, proc_src, proc_dest, w_node, out_grad
):
    smem = pl.BlockSpec(memory_space=pltpu.SMEM)
    hbm = pl.BlockSpec(memory_space=pl.ANY)
    vmem = pl.BlockSpec(memory_space=pltpu.VMEM)
    V = pltpu.VMEM
    dma = pltpu.SemaphoreType.DMA
    return pl.pallas_call(
        kernel,
        out_shape=(
            jax.ShapeDtypeStruct((MR, W), BF),
            jax.ShapeDtypeStruct((MR, W), F32),
            jax.ShapeDtypeStruct((C_IN, W), F32),
            jax.ShapeDtypeStruct((LAT, W), F32),
        ),
        in_specs=[smem] + [vmem] * 4 + [hbm] * 7,
        out_specs=(vmem,) * 4,
        scratch_shapes=[
            V((NB, C_IN, W), BF),
            V((T, CP, W), BF),
            V((CP, ER), BF),
            V((LAT, CP), BF),
            V((C_IN, W), BF),
            V((MR, LAT), BF),
            V((LAT, W), BF),
            V((W, LAT), BF),
            V((MR, W), BF),
            V((EP * W, W), BF),
            V((PP * W, W), BF),
            V((EP * W, W), F32),
            V((CELLS * W, W), F32),
            V((MR, ER), BF),
            V((MR, 3 * MR), BF),
            V((3 * MR, MR), BF),
            V((MR, W), F32),
            V((LAT, ER), F32),
            V((MR, LAT), BF),
            V((MR, LAT), F32),
            V((MR, W), F32),
            V((NX, MR, W), BF),
            V((3 * MR, W), BF),
            V((MR, LAT), BF),
            V((2, MR, W), BF),
            V((2, MR, W), BF),
            V((MR, W), F32),
            V((W, LAT), F32),
            V((LAT, W), F32),
            V((LAT, MR), BF),
            V((2 * W, ER), BF),
            V((CP, 2 * W), F32),
            V((CP, LAT), BF),
            V((NX, CP, W), BF),
            V((2, 512, W), F32),
            V((2, 256, W), F32),
            V((NT, 16, W), BF),
            V((NT, 16, W), BF),
            V((NT, 16, W), BF),
            V((NT, 16, W), BF),
            dma((7,)),
            dma((NB,)),
            dma((T,)), dma((T,)),
            dma((3, NX)), dma((3, NX)),
            dma((2,)), dma((2,)),
            dma((2,)), dma((2,)),
            dma((5, NX)), dma((5, NX)),
            dma((2,)), dma((2,)),
            dma((2, NT)), dma((2, NT)),
        ],
        compiler_params=pltpu.CompilerParams(
            collective_id=0, has_side_effects=True, vmem_limit_bytes=60 << 20
        ),
    )(
        send_order, enc_slot, enc_dest, proc_src, proc_dest,
        grid_in.T, w_embed, enc_coef.reshape(EP * W, W), mesh_in,
        proc_coef.reshape(PP * W, W), w_node, out_grad,
    )


def solution(mesh):
    return jax.shard_map(
        on_device,
        mesh=mesh,
        in_specs=(
            P("band", None),
            P(None, "chan"),
            P("band", None),
            P("band", None, None),
            P("band", None),
            P("band", None),
            P("band", "chan"),
            P("band", None, None),
            P("band", None),
            P("band", None),
            P(None, "chan"),
            P("band", "chan"),
        ),
        out_specs=(P("band", "chan"), P("band", "chan"), P(None, "chan"), P(None, "chan")),
        check_vma=False,
    )
```

```python
import jax
import jax.numpy as jnp
from jax import lax
from jax.experimental import pallas as pl
from jax.experimental.pallas import tpu as pltpu
from jax.sharding import PartitionSpec as P

MESH = pl.DeviceIdType.MESH
F32 = jnp.float32
BF = jnp.bfloat16
NB = 64
NX = 4
C_IN = 474
CP = 480
LAT = 512
W = 128
T = NB // NX
EP = 96
PP = 48
MB = 5
MR = MB * W
ER = T * W
CELLS = MB * T
LATE = 4
LATE_CELLS = MB * NX * LATE
FIRST = 4
ZS = 8
YS = 4
ZR = 32
HALF = CP // 2


def dot(a, b):
    return jnp.dot(a, b, preferred_element_type=F32)


def slope_of(v, s):
    return s * (1.0 + v * (1.0 - s))


def al(v, m):
    return pl.multiple_of(v, m)


def finish(out_in, grad_in, fin, fin2, node_fin, node_fin2, mesh_out, mesh_grad, gemb, gnode):
    core = lax.rem(lax.axis_index("band"), 2)
    mesh_out[...] = out_in[...]
    mesh_grad[...] = grad_in[...]
    gnode[pl.ds(al(core * 256, 256), 256), :] = node_fin[...].reshape(256, W)
    gnode[pl.ds(al((1 - core) * 256, 256), 256), :] = node_fin2[...].reshape(256, W)

    def write(low, high):
        gemb[0:HALF, :] = low[...].reshape(256, W)[:HALF].astype(F32)
        gemb[HALF:C_IN, :] = high[...].reshape(256, W)[: C_IN - HALF].astype(F32)

    @pl.when(core == 0)
    def _():
        write(fin, fin2)

    @pl.when(core == 1)
    def _():
        write(fin2, fin)


def kernel(
    order, eslot, edest, psrc, pdest, grid, wemb, ecoef, meshin, pcoef, wnode, ograd,
    mesh_out, mesh_grad, fin_out, fin2_out, node_out, node2_out,
    flat, flat_last, blocks, stage, recv, we_all, wtmp, og_all, wn, wr_all, mi, ce,
    wide, cells, a_enc, a_late, a_proc, at_proc, gh, slope,
    part, enc_sum, enc_slope_f, rs1, lat_out, lat_in, ext, hid_all, hb_out, hb_in, mid, gn_out, gn_in, ge_all, gp,
    half_f, half_out, half_in, gemb_out, rs2, node_in, pieces_e, pieces_n, landed_e, landed_n, by_y, fin_e, fin_e2, fin_n, fin_n2, mo, mg,
    lsem, g_s, f_s, f_r, a_s, a_r, x_s, x_r, h_s, h_r, b_s, b_r, c_s, c_r, t_s, t_r, u_s, u_r, v_s, v_r, l_s, l_r,
):
    me = lax.axis_index("band")
    x = lax.axis_index("chan")
    core = lax.rem(me, 2)
    chip = lax.div(me, 2)
    mine = pl.ds(al(x * W, W), W)

    def to_band(src, dst, ss, rs, band):
        return pltpu.make_async_remote_copy(src, dst, ss, rs, device_id={"band": band}, device_id_type=MESH)

    def to_chan(src, dst, ss, rs, chan):
        return pltpu.make_async_remote_copy(src, dst, ss, rs, device_id={"chan": chan}, device_id_type=MESH)

    def peer(dx):
        return lax.rem(x + dx, NX)

    def cols(c):
        return pl.ds(al(c * W, W), W)

    def rows_of(c):
        return pl.ds(al(c * W, W), W)

    steps = ((0, 128), (128, 256), (256, 384), (384, C_IN))
    load_grid = [
        pltpu.make_async_copy(grid.at[a:b, :], flat_last if i == 3 else flat.at[i % 2], g_s.at[i])
        for i, (a, b) in enumerate(steps)
    ]
    for i in (0, 1, 3):
        load_grid[i].start()
    load_wemb = pltpu.make_async_copy(wemb, wtmp, lsem.at[1])
    load_og = pltpu.make_async_copy(ograd, og_all.at[:, mine], lsem.at[2])
    load_wn = pltpu.make_async_copy(wnode, wn, lsem.at[3])
    load_mi = pltpu.make_async_copy(meshin, mi, lsem.at[4])
    load_ce = pltpu.make_async_copy(ecoef, ce, lsem.at[5])
    cp = ce.at[0 : PP * W, :]
    load_cp = pltpu.make_async_copy(pcoef, cp, lsem.at[6])
    load_wemb.start()
    load_og.start()
    load_wn.start()

    barrier = pltpu.get_barrier_semaphore()

    def greet(band):
        pl.semaphore_signal(barrier, inc=1, device_id={"band": band}, device_id_type=MESH)

    z_here = lax.div(me, 8)
    y_here = lax.rem(chip, YS)
    has_low = me > 0
    has_high = me < NB - 1
    low = lax.rem(me + NB - 1, NB)
    high = lax.rem(me + 1, NB)
    sibling = me + 1 - 2 * core

    def at_z(j):
        return lax.rem(me + 8 * j, NB)

    def at_y(j):
        return z_here * 8 + lax.rem(y_here + j, YS) * 2 + core

    def greet_source(t, _):
        @pl.when(x + t != 0)
        def _():
            greet(lax.rem(me - x - NX * t + 2 * NB, NB))

        return 0

    lax.fori_loop(0, T, greet_source, 0)
    pl.when(has_low)(lambda: greet(low))
    pl.when(has_high)(lambda: greet(high))
    greet(sibling)
    for j in range(1, ZS):
        greet(at_z(j))
    for j in range(1, YS):
        greet(at_y(j))
    for dx in range(1, NX):
        pl.semaphore_signal(barrier, inc=1, device_id={"chan": peer(dx)}, device_id_type=MESH)
    greetings = T + 2 + 1 + ZS - 1 + YS - 1 + NX - 1
    absent = jnp.where(x == 0, 1, 0) + jnp.where(me == 0, 1, 0) + jnp.where(me == NB - 1, 1, 0)

    stage[:, CP - 16 :, :] = jnp.zeros((T, 16, W), BF)
    def band_of(t):
        return lax.rem(me + x + NX * t, NB)

    def first_copy(t):
        rows = pl.ds(0, W)
        return to_band(stage.at[t, rows, :], recv.at[rows, cols(t)], f_s.at[t], f_r.at[t], band_of(t))

    def rest_copy(t):
        rows = pl.ds(W, CP - W)
        return to_band(stage.at[t, rows, :], recv.at[rows, cols(t)], a_s.at[t], a_r.at[t], band_of(t))

    def grid_copy(t):
        return to_band(stage.at[t], recv.at[:, cols(t)], a_s.at[t], a_r.at[t], band_of(t))

    def over_slots(lo, hi, body):
        def one(t, _):
            pl.when(x + t != 0)(lambda: body(t))
            return 0

        lax.fori_loop(lo, hi, one, 0)

    for i, (a, b) in enumerate(steps):
        load_grid[i].wait()

        def by_block(k, _, i=i, n=b - a):
            blocks[k, 0:n, :] = flat_last[:, cols(k)] if i == 3 else flat[i % 2, :, cols(k)]
            return 0

        lax.fori_loop(0, NB, by_block, 0, unroll=4)
        if i == 0:
            load_grid[2].start()

        def to_stage(t, _, a=a, b=b):
            stage[t, a:b, :] = blocks[order[0, band_of(t)], 0 : b - a, :]
            return 0

        lax.fori_loop(0, T, to_stage, 0, unroll=2)
        if i == 0:
            pl.semaphore_wait(barrier, greetings - absent)
            over_slots(0, FIRST, lambda t: first_copy(t).start())
    over_slots(0, FIRST, lambda t: rest_copy(t).start())
    over_slots(FIRST, T - LATE, lambda t: grid_copy(t).start())
    load_mi.start()
    load_ce.start()

    @pl.when(x == 0)
    def _():
        recv[:, 0:W] = stage[0]

    load_wemb.wait()
    we_all[mine, CP - W : CP] = jnp.zeros((W, W), BF)
    we_all[mine, :C_IN] = wtmp[...].astype(F32).T.astype(BF)
    load_og.wait()
    load_wn.wait()
    wr_all[:, mine] = wn[mine, :]

    def early(dx):
        p = peer(dx)
        return (
            to_chan(we_all.at[mine, :], we_all.at[mine, :], x_s.at[0, dx], x_r.at[0, dx], p),
            to_chan(og_all.at[:, mine], og_all.at[:, mine], x_s.at[1, dx], x_r.at[1, dx], p),
            to_chan(wn.at[rows_of(p), :], wr_all.at[:, mine], x_s.at[2, dx], x_r.at[2, dx], p),
        )

    for dx in range(1, NX):
        for c in early(dx):
            c.start()

    def sum_cells(coef, pairs, count, hits):
        wide[0 : pairs * W, :] = coef[...].astype(F32)
        pick = jnp.where(hits, 1.0, 0.0).astype(BF)

        def one(i, _):
            line = wide[pl.ds(i, pairs, stride=W), :].astype(BF)
            cells[pl.ds(i, count, stride=W), :] = dot(pick, line)
            return 0

        lax.fori_loop(0, W, one, 0, unroll=4)

    def cell_ids(pairs):
        cell = lax.broadcasted_iota(jnp.int32, (CELLS, pairs), 0)
        return lax.shift_right_logical(cell, 4), lax.bitwise_and(cell, T - 1)

    load_ce.wait()
    cell = lax.broadcasted_iota(jnp.int32, (CELLS + LATE_CELLS, EP), 0)
    tail = cell - CELLS
    own_group = cell < CELLS
    cell_m = jnp.where(own_group, lax.shift_right_logical(cell, 4), lax.shift_right_arithmetic(tail, 4))
    cell_t = jnp.where(own_group, lax.bitwise_and(cell, T - 1), T - LATE + lax.bitwise_and(tail, LATE - 1))
    cell_x = jnp.where(own_group, x, lax.bitwise_and(lax.shift_right_arithmetic(tail, 2), NX - 1))
    cell_slot = lax.bitwise_and(me - cell_x - NX * cell_t + 2 * NB, NB - 1)
    sum_cells(ce, EP, CELLS + LATE_CELLS, (edest[...] == cell_m) & (eslot[...] == cell_slot))

    load_cp.start()

    def enc_cells(t, _):
        for m in range(MB):
            a_enc[m * W : (m + 1) * W, cols(t)] = cells[rows_of(m * T + t), :].astype(BF)
        return 0

    lax.fori_loop(0, T, enc_cells, 0)

    def late_cells(t, _):
        for m in range(MB):
            a_late[m * W : (m + 1) * W, cols(t)] = cells[rows_of(CELLS + m * NX * LATE + t), :].astype(BF)
        return 0

    lax.fori_loop(0, NX * LATE, late_cells, 0)

    load_cp.wait()
    cell_m, cell_s = cell_ids(PP)
    sum_cells(cp, PP, CELLS, (pdest[...] == cell_m) & (psrc[...] == cell_s))

    def proc_cells(s, _):
        for m in range(MB):
            block = cells[rows_of(m * T + s), :]
            a_proc[m * W : (m + 1) * W, cols(s)] = block.astype(BF)
            at_proc[rows_of(s), m * W : (m + 1) * W] = block.T.astype(BF)
        return 0

    lax.fori_loop(0, 3 * MB, proc_cells, 0)

    for dx in range(1, NX):
        for c in early(dx):
            c.wait_recv()
    gh[...] = lax.dot_general(og_all[...], wr_all[...], (((1,), (1,)), ((), ())), preferred_element_type=F32)

    def sent_first(t):
        first_copy(t).wait_send()
        rest_copy(t).wait_send()

    over_slots(0, FIRST, sent_first)
    over_slots(FIRST, T - LATE, lambda t: grid_copy(t).wait_send())
    over_slots(T - LATE, T, lambda t: grid_copy(t).start())

    def dot_nt(a, b):
        return lax.dot_general(a, b, (((1,), (1,)), ((), ())), preferred_element_type=F32)

    enc_sum[...] = jnp.zeros((MR, LAT), F32)

    def embed(u):
        here = pl.ds(al(u * 2 * W, 2 * W), 2 * W)
        pre = dot(we_all[...], recv[:, here])
        sig = jax.nn.sigmoid(pre)
        slope[:, here] = slope_of(pre, sig)
        return (pre * sig).astype(BF), here

    def embed_sum(u, _):
        latent, here = embed(u)
        enc_sum[...] += dot_nt(a_enc[:, here], latent)
        return 0

    def first_slots(u, _):
        def arrive(t):
            first_copy(t).wait_recv()
            rest_copy(t).wait_recv()

        over_slots(2 * u, 2 * u + 2, arrive)
        return embed_sum(u, 0)

    def other_slots(u, _):
        over_slots(2 * u, 2 * u + 2, lambda t: grid_copy(t).wait_recv())
        return embed_sum(u, 0)

    lax.fori_loop(0, FIRST // 2, first_slots, 0)
    lax.fori_loop(FIRST // 2, (T - LATE) // 2, other_slots, 0)

    half = lax.div(x, 2)
    away = 1 - half
    twin = x + 1 - 2 * lax.rem(x, 2)
    far = (2 * away, 2 * away + 1)

    def two(h):
        return pl.ds(al(h * 2 * W, 2 * W), 2 * W)

    def enc_copy(c):
        return to_chan(part.at[:, cols(c)], rs1.at[x], c_s.at[0, c], c_r.at[0, x], c)

    part[:, two(away)] = enc_sum[:, two(away)].astype(BF)
    for c in far:
        enc_copy(c).start()
    part[:, cols(twin)] = enc_sum[:, cols(twin)].astype(BF)
    enc_copy(twin).start()

    def late_copy(v, c):
        return to_chan(lat_out.at[v, rows_of(c), :], lat_in.at[x, v], l_s.at[v, c], l_r.at[v, x], c)

    for v in range(LATE // 2):
        t = T - LATE + 2 * v
        over_slots(t, t + 2, lambda t: grid_copy(t).wait_recv())
        lat_out[v] = embed(t // 2)[0]
        for c in (*far, twin):
            late_copy(v, c).start()
    load_mi.wait()

    def late_sum(c):
        out = jnp.zeros((MR, W), F32)
        for v in range(LATE // 2):
            here = pl.ds(al((c * LATE + 2 * v) * W, 2 * W), 2 * W)
            out = out + dot_nt(a_late[:, here], lat_in[c, v])
        return out

    lat_in[x] = lat_out[:, mine, :]
    enc_pre = enc_sum[:, mine] + late_sum(x)
    for dx in range(1, NX):
        p = peer(dx)
        to_chan(part.at[:, cols(p)], rs1.at[p], c_s.at[0, p], c_r.at[0, p], p).wait_recv()
        enc_pre = enc_pre + rs1[p].astype(F32)
    for c in (twin, *far):
        for v in range(LATE // 2):
            to_chan(lat_out.at[v, rows_of(c), :], lat_in.at[c, v], l_s.at[v, c], l_r.at[v, c], c).wait_recv()
        enc_pre = enc_pre + late_sum(c)
    enc_sig = jax.nn.sigmoid(enc_pre)
    mesh_one = (mi[...].astype(F32) + enc_pre * enc_sig).astype(BF)
    enc_slope = slope_of(enc_pre, enc_sig)
    enc_slope_f[...] = enc_slope

    ext[MR : 2 * MR, :] = mesh_one
    own_ext = ext.at[MR : 2 * MR, :]
    halo_up = to_band(own_ext, ext.at[0:MR, :], h_s.at[0], h_r.at[0], high)
    halo_down = to_band(own_ext, ext.at[2 * MR : 3 * MR, :], h_s.at[1], h_r.at[1], low)
    pl.when(has_high)(halo_up.start)
    pl.when(has_low)(halo_down.start)
    mid[...] = dot(a_proc[:, MR : 2 * MR], mesh_one)

    @pl.when(me == 0)
    def _():
        ext[0:MR, :] = jnp.zeros((MR, W), BF)

    @pl.when(me == NB - 1)
    def _():
        ext[2 * MR : 3 * MR, :] = jnp.zeros((MR, W), BF)

    pl.when(has_low)(halo_up.wait_recv)
    pl.when(has_high)(halo_down.wait_recv)
    proc_pre = (
        mid[...]
        + dot(a_proc[:, 0:MR], ext[0:MR, :])
        + dot(a_proc[:, 2 * MR : 3 * MR], ext[2 * MR : 3 * MR, :])
    )
    proc_sig = jax.nn.sigmoid(proc_pre)
    hidden = (proc_pre * proc_sig).astype(BF)
    hid_all[:, mine] = hidden

    def hid_copy(c):
        return to_chan(hid_all.at[:, mine], hid_all.at[:, mine], c_s.at[1, c], c_r.at[1, x], c)

    grad_proc = (gh[...] * slope_of(proc_pre, proc_sig)).astype(BF)

    hb_out[0] = dot(at_proc[0:MR, :], grad_proc).astype(BF)
    back_down = to_band(hb_out.at[0], hb_in.at[0], b_s.at[0], b_r.at[0], low)
    pl.when(has_low)(back_down.start)
    hb_out[1] = dot(at_proc[2 * MR : 3 * MR, :], grad_proc).astype(BF)
    back_up = to_band(hb_out.at[1], hb_in.at[1], b_s.at[1], b_r.at[1], high)
    pl.when(has_high)(back_up.start)
    mid[...] = dot(at_proc[MR : 2 * MR, :], grad_proc) + og_all[:, mine].astype(F32)

    gn_out[...] = dot(hidden.astype(F32).T.astype(BF), og_all[...])
    gn_in[mine, :] = gn_out[:, mine]

    def gn_copy(c):
        return to_chan(gn_out.at[:, cols(c)], gn_in.at[mine, :], c_s.at[2, c], c_r.at[2, x], c)

    for dx in range(1, NX):
        gn_copy(peer(dx)).start()

    @pl.when(me == NB - 1)
    def _():
        hb_in[0] = jnp.zeros((MR, W), BF)

    @pl.when(me == 0)
    def _():
        hb_in[1] = jnp.zeros((MR, W), BF)

    pl.when(has_high)(back_down.wait_recv)
    pl.when(has_low)(back_up.wait_recv)
    total = mid[...] + hb_in[0].astype(F32) + hb_in[1].astype(F32)
    mg[...] = total
    save_grad = pltpu.make_async_copy(mg, mesh_grad, lsem.at[1])
    save_grad.start()
    ge_all[mine, :] = (total * enc_slope_f[...]).T.astype(BF)

    def ge_copy(c):
        return to_chan(ge_all.at[mine, :], ge_all.at[mine, :], c_s.at[3, c], c_r.at[3, x], c)

    def ge_wait(c):
        to_chan(ge_all.at[rows_of(c), :], ge_all.at[rows_of(c), :], c_s.at[3, c], c_r.at[3, c], c).wait_recv()

    for c in (twin, *far):
        ge_copy(c).start()

    keep = pl.ds(al(core * 256, 256), 256)
    give = pl.ds(al((1 - core) * 256, 256), 256)
    pieces = (pieces_e, pieces_n)
    landed = (landed_e, landed_n)
    result = (fin_e, fin_n)
    other = (fin_e2, fin_n2)

    def z_of(j):
        return lax.rem(z_here + j, ZS)

    def sum_z(k, j):
        return to_band(pieces[k].at[z_of(j)], landed[k].at[z_here], u_s.at[k, j], u_r.at[k, j], at_z(j))

    def sum_y(k, j):
        return to_band(by_y.at[k, y_here], by_y.at[k, y_here], v_s.at[k, j], v_r.at[k, j], at_y(j))

    def back_z(k, j):
        return to_band(result[k].at[z_here], result[k].at[z_here], u_s.at[2 + k, j], u_r.at[2 + k, j], at_z(j))

    def start_z(k):
        for j in range(1, ZS):
            sum_z(k, j).start()
        landed[k][z_here] = pieces[k][z_here]

    def start_y(k):
        for j in range(1, ZS):
            sum_z(k, j).wait_recv()
        by_y[k, y_here] = jnp.sum(landed[k][...].astype(F32), axis=0)
        for j in range(1, YS):
            sum_y(k, j).start()

    def start_back(k):
        for j in range(1, YS):
            y = lax.rem(y_here - j + YS, YS)
            to_band(by_y.at[k, y], by_y.at[k, y], v_s.at[k, j], v_r.at[k, j], at_y(j)).wait_recv()
        result[k][z_here] = jnp.sum(by_y[k], axis=0).astype(result[k].dtype)
        for j in range(1, ZS):
            back_z(k, j).start()

    def swap_back(k):
        for j in range(1, ZS):
            z = lax.rem(z_here - j + ZS, ZS)
            to_band(result[k].at[z], result[k].at[z], u_s.at[2 + k, j], u_r.at[2 + k, j], at_z(j)).wait_recv()
        copy = to_band(result[k], other[k], t_s.at[2 + k], t_r.at[2 + k], sibling)
        copy.start()
        return copy

    for dx in range(1, NX):
        p = peer(dx)
        prow = pl.ds(al(p * W, W), W)
        to_chan(gn_out.at[:, cols(p)], gn_in.at[prow, :], c_s.at[2, p], c_r.at[2, p], p).wait_recv()
    node_swap = to_band(gn_in.at[give, :], node_in, t_s.at[0], t_r.at[0], sibling)
    node_swap.start()
    node_swap.wait_recv()
    pieces_n[...] = (gn_in[keep, :] + node_in[...]).reshape(ZS, ZR, W)
    start_z(1)

    gemb_f = enc_sum.at[0:CP, 0 : 2 * W]

    def back(h):
        def piece(t, _):
            here = pl.ds(al(t * 512, 512), 512)
            msg = dot(ge_all[two(h), :], a_enc[:, here])
            gp[:, here] = (msg * slope[two(h), here]).astype(BF)
            return 0

        lax.fori_loop(0, ER // 512, piece, 0)
        gemb_f[...] = dot_nt(recv[...], gp[...])

    keep_rows = pl.ds(al(core * HALF, 16), HALF)
    give_rows = pl.ds(al((1 - core) * HALF, 16), HALF)

    def half_copy(k):
        return to_band(half_out.at[k], half_in.at[k], h_s.at[2 + k], h_r.at[2 + k], sibling)

    def ge2_copy(c):
        return to_chan(gemb_out.at[:, cols(c)], rs2.at[x], c_s.at[4, c], c_r.at[4, x], c)

    ge_wait(twin)
    back(half)
    half_out[0] = gemb_f[give_rows, :]
    half_copy(0).start()
    half_f[0] = gemb_f[keep_rows, :]
    start_y(1)
    for c in far:
        ge_wait(c)
    back(away)
    half_out[1] = gemb_f[give_rows, :]
    half_copy(1).start()
    half_f[1] = gemb_f[keep_rows, :]
    half_copy(0).wait_recv()
    half_f[0] = half_f[0] + half_in[0]
    gemb_out[:, two(half)] = half_f[0].astype(BF)
    ge2_copy(twin).start()
    half_copy(1).wait_recv()
    gemb_out[:, two(away)] = (half_f[1] + half_in[1]).astype(BF)
    for c in far:
        ge2_copy(c).start()
    for dx in range(1, NX):
        hid_copy(peer(dx)).start()
    start_back(1)
    total = half_f[0, :, pl.ds(al(lax.rem(x, 2) * W, W), W)]
    for dx in range(1, NX):
        p = peer(dx)
        to_chan(gemb_out.at[:, cols(p)], rs2.at[p], c_s.at[4, p], c_r.at[4, p], p).wait_recv()
        total = total + rs2[p].astype(F32)
    padded = jnp.concatenate([total, jnp.zeros((ZS * ZR - HALF, W), F32)], axis=0)
    pieces_e[...] = padded.astype(BF).reshape(ZS, ZR, W)
    start_z(0)
    node_back = swap_back(1)
    start_y(0)
    start_back(0)

    for dx in range(1, NX):
        p = peer(dx)
        to_chan(hid_all.at[:, cols(p)], hid_all.at[:, cols(p)], c_s.at[1, p], c_r.at[1, p], p).wait_recv()
    mo[...] = (ext[MR : 2 * MR, :].astype(F32) + dot(hid_all[...], wn[...])).astype(BF)
    save_out = pltpu.make_async_copy(mo, mesh_out, lsem.at[2])
    save_out.start()
    node_back.wait_recv()
    node_saves = [pltpu.make_async_copy(fin_n, node_out, lsem.at[3]), pltpu.make_async_copy(fin_n2, node2_out, lsem.at[4])]
    for c in node_saves:
        c.start()
    last_back = swap_back(0)
    last_save = pltpu.make_async_copy(fin_e, fin_out, lsem.at[5])
    last_save.start()
    last_back.wait_recv()
    last_save2 = pltpu.make_async_copy(fin_e2, fin2_out, lsem.at[6])
    last_save2.start()
    saves = (*node_saves, last_save, last_save2)

    over_slots(T - LATE, T, lambda t: grid_copy(t).wait_send())
    for dx in range(1, NX):
        p = peer(dx)
        for c in early(dx):
            c.wait_send()
        for v in range(LATE // 2):
            late_copy(v, p).wait_send()
        for f in (enc_copy, hid_copy, gn_copy, ge_copy, ge2_copy):
            f(p).wait_send()
    pl.when(has_high)(halo_up.wait_send)
    pl.when(has_low)(halo_down.wait_send)
    pl.when(has_low)(back_down.wait_send)
    pl.when(has_high)(back_up.wait_send)
    for k in range(2):
        half_copy(k).wait_send()
    for c in (node_swap, node_back, last_back):
        c.wait_send()

    for k in range(2):
        for j in range(1, ZS):
            sum_z(k, j).wait_send()
            back_z(k, j).wait_send()
        for j in range(1, YS):
            sum_y(k, j).wait_send()
    save_grad.wait()
    save_out.wait()
    for c in saves:
        c.wait()


def on_device(
    grid_in, w_embed, send_order, enc_coef, enc_slot, enc_dest, mesh_in, proc_coef, proc_src, proc_dest, w_node, out_grad
):
    smem = pl.BlockSpec(memory_space=pltpu.SMEM)
    hbm = pl.BlockSpec(memory_space=pl.ANY)
    vmem = pl.BlockSpec(memory_space=pltpu.VMEM)
    V = pltpu.VMEM
    dma = pltpu.SemaphoreType.DMA
    piece = jax.ShapeDtypeStruct((ZS, ZR, W), F32)
    piece_bf = jax.ShapeDtypeStruct((ZS, ZR, W), BF)
    parts = pl.pallas_call(
        kernel,
        out_shape=(
            jax.ShapeDtypeStruct((MR, W), BF),
            jax.ShapeDtypeStruct((MR, W), F32),
            piece_bf, piece_bf, piece, piece,
        ),
        in_specs=[smem] + [vmem] * 4 + [hbm] * 7,
        out_specs=(hbm,) * 6,
        scratch_shapes=[
            V((2, W, NB * W), BF),
            V((C_IN - 3 * W, NB * W), BF),
            V((NB, W, W), BF),
            V((T, CP, W), BF),
            V((CP, ER), BF),
            V((LAT, CP), BF),
            V((C_IN, W), BF),
            V((MR, LAT), BF),
            V((LAT, W), BF),
            V((W, LAT), BF),
            V((MR, W), BF),
            V((EP * W, W), BF),
            V((EP * W, W), F32),
            V(((CELLS + LATE_CELLS) * W, W), F32),
            V((MR, ER), BF),
            V((MR, NX * LATE * W), BF),
            V((MR, 3 * MR), BF),
            V((3 * MR, MR), BF),
            V((MR, W), F32),
            V((LAT, ER), F32),
            V((MR, LAT), BF),
            V((MR, LAT), F32),
            V((MR, W), F32),
            V((NX, MR, W), BF),
            V((LATE // 2, LAT, 2 * W), BF),
            V((NX, LATE // 2, W, 2 * W), BF),
            V((3 * MR, W), BF),
            V((MR, LAT), BF),
            V((2, MR, W), BF),
            V((2, MR, W), BF),
            V((MR, W), F32),
            V((W, LAT), F32),
            V((LAT, W), F32),
            V((LAT, MR), BF),
            V((2 * W, ER), BF),
            V((2, HALF, 2 * W), F32),
            V((2, HALF, 2 * W), F32),
            V((2, HALF, 2 * W), F32),
            V((HALF, LAT), BF),
            V((NX, HALF, W), BF),
            V((256, W), F32),
            V((ZS, ZR, W), BF),
            V((ZS, ZR, W), F32),
            V((ZS, ZR, W), BF),
            V((ZS, ZR, W), F32),
            V((2, YS, ZR, W), F32),
            V((ZS, ZR, W), BF),
            V((ZS, ZR, W), BF),
            V((ZS, ZR, W), F32),
            V((ZS, ZR, W), F32),
            V((MR, W), BF),
            V((MR, W), F32),
            dma((7,)),
            dma((4,)),
            dma((FIRST,)), dma((FIRST,)),
            dma((T,)), dma((T,)),
            dma((3, NX)), dma((3, NX)),
            dma((4,)), dma((4,)),
            dma((2,)), dma((2,)),
            dma((5, NX)), dma((5, NX)),
            dma((4,)), dma((4,)),
            dma((4, ZS)), dma((4, ZS)),
            dma((2, YS)), dma((2, YS)),
            dma((LATE // 2, NX)), dma((LATE // 2, NX)),
        ],
        compiler_params=pltpu.CompilerParams(
            collective_id=0, has_side_effects=True, vmem_limit_bytes=60 << 20
        ),
    )(
        send_order, enc_slot, enc_dest, proc_src, proc_dest, grid_in.T,
        w_embed, enc_coef.reshape(EP * W, W), mesh_in,
        proc_coef.reshape(PP * W, W), w_node, out_grad,
    )
    return pl.pallas_call(
        finish,
        out_shape=(
            jax.ShapeDtypeStruct((MR, W), BF),
            jax.ShapeDtypeStruct((MR, W), F32),
            jax.ShapeDtypeStruct((C_IN, W), F32),
            jax.ShapeDtypeStruct((LAT, W), F32),
        ),
        in_specs=[vmem] * 6,
        out_specs=(vmem,) * 4,
        compiler_params=pltpu.CompilerParams(vmem_limit_bytes=60 << 20),
    )(*parts)


def solution(mesh):
    return jax.shard_map(
        on_device,
        mesh=mesh,
        in_specs=(
            P("band", None),
            P(None, "chan"),
            P("band", None),
            P("band", None, None),
            P("band", None),
            P("band", None),
            P("band", "chan"),
            P("band", None, None),
            P("band", None),
            P("band", None),
            P(None, "chan"),
            P("band", "chan"),
        ),
        out_specs=(P("band", "chan"), P("band", "chan"), P(None, "chan"), P(None, "chan")),
        check_vma=False,
    )
```

```python
import jax
import jax.numpy as jnp
from jax import lax
from jax.experimental import pallas as pl
from jax.experimental.pallas import tpu as pltpu
from jax.sharding import PartitionSpec as P

MESH = pl.DeviceIdType.MESH
F32 = jnp.float32
BF = jnp.bfloat16
NB = 64
NX = 4
C_IN = 474
CP = 480
LAT = 512
W = 128
T = NB // NX
EP = 96
PP = 48
MB = 5
MR = MB * W
ER = T * W
CELLS = MB * T
LATE = 2
LATE_CELLS = MB * NX * LATE
OWN = 1
FIRST = 4
ZS = 8
YS = 4
ZR = 32
HALF = CP // 2


def place_of(t):
    return (3 * t + 13) & (T - 1)


def dot(a, b):
    return jnp.dot(a, b, preferred_element_type=F32)


def slope_of(v, s):
    return s * (1.0 + v * (1.0 - s))


def al(v, m):
    return pl.multiple_of(v, m)


def finish(out_in, grad_in, fin, fin2, node_fin, node_fin2, mesh_out, mesh_grad, gemb, gnode):
    core = lax.rem(lax.axis_index("band"), 2)
    mesh_out[...] = out_in[...]
    mesh_grad[...] = grad_in[...]
    gnode[pl.ds(al(core * 256, 256), 256), :] = node_fin[...].reshape(256, W)
    gnode[pl.ds(al((1 - core) * 256, 256), 256), :] = node_fin2[...].reshape(256, W)

    def write(low, high):
        gemb[0:HALF, :] = low[...].reshape(256, W)[:HALF].astype(F32)
        gemb[HALF:C_IN, :] = high[...].reshape(256, W)[: C_IN - HALF].astype(F32)

    @pl.when(core == 0)
    def _():
        write(fin, fin2)

    @pl.when(core == 1)
    def _():
        write(fin2, fin)


def kernel(
    order, eslot, edest, psrc, pdest, grid, wemb, ecoef, meshin, pcoef, wnode, ograd,
    mesh_out, mesh_grad, fin_out, fin2_out, node_out, node2_out,
    flat, flat_last, blocks, stage, recv, we_all, wtmp, og_all, wn, wr_all, mi, ce,
    wide, cells, a_enc, a_late, a_proc, at_proc, gh, slope,
    part, enc_sum, enc_slope_f, rs1, lat_out, lat_in, ext, hid_all, hb_out, hb_in, mid, gn_out, gn_in, ge_all, gp,
    half_f, half_out, half_in, gemb_out, rs2, node_in, pieces_e, pieces_n, landed_e, landed_n, by_y, fin_e, fin_e2, fin_n, fin_n2, mo, mg,
    lsem, g_s, f_s, f_r, a_s, a_r, x_s, x_r, h_s, h_r, b_s, b_r, c_s, c_r, t_s, t_r, u_s, u_r, v_s, v_r, l_s, l_r,
):
    me = lax.axis_index("band")
    x = lax.axis_index("chan")
    core = lax.rem(me, 2)
    chip = lax.div(me, 2)
    mine = pl.ds(al(x * W, W), W)

    def to_band(src, dst, ss, rs, band):
        return pltpu.make_async_remote_copy(src, dst, ss, rs, device_id={"band": band}, device_id_type=MESH)

    def to_chan(src, dst, ss, rs, chan):
        return pltpu.make_async_remote_copy(src, dst, ss, rs, device_id={"chan": chan}, device_id_type=MESH)

    def peer(dx):
        return lax.rem(x + dx, NX)

    def cols(c):
        return pl.ds(al(c * W, W), W)

    def rows_of(c):
        return pl.ds(al(c * W, W), W)

    steps = ((0, 128), (128, 256), (256, 384), (384, C_IN))
    load_grid = [
        pltpu.make_async_copy(grid.at[a:b, :], flat_last if i == 3 else flat.at[i % 2], g_s.at[i])
        for i, (a, b) in enumerate(steps)
    ]
    for i in (0, 1, 3):
        load_grid[i].start()
    load_wemb = pltpu.make_async_copy(wemb, wtmp, lsem.at[1])
    load_og = pltpu.make_async_copy(ograd, og_all.at[:, mine], lsem.at[2])
    load_wn = pltpu.make_async_copy(wnode, wn, lsem.at[3])
    load_mi = pltpu.make_async_copy(meshin, mi, lsem.at[4])
    load_ce = pltpu.make_async_copy(ecoef, ce, lsem.at[5])
    cp = ce.at[0 : PP * W, :]
    load_cp = pltpu.make_async_copy(pcoef, cp, lsem.at[6])
    load_wemb.start()
    load_og.start()
    load_wn.start()

    barrier = pltpu.get_barrier_semaphore()

    def greet(band):
        pl.semaphore_signal(barrier, inc=1, device_id={"band": band}, device_id_type=MESH)

    z_here = lax.div(me, 8)
    y_here = lax.rem(chip, YS)
    has_low = me > 0
    has_high = me < NB - 1
    low = lax.rem(me + NB - 1, NB)
    high = lax.rem(me + 1, NB)
    sibling = me + 1 - 2 * core

    def at_z(j):
        return lax.rem(me + 8 * j, NB)

    def at_y(j):
        return z_here * 8 + lax.rem(y_here + j, YS) * 2 + core

    def greet_source(t, _):
        @pl.when(x + t != 0)
        def _():
            greet(lax.rem(me - x - NX * t + 2 * NB, NB))

        return 0

    lax.fori_loop(0, T, greet_source, 0)
    pl.when(has_low)(lambda: greet(low))
    pl.when(has_high)(lambda: greet(high))
    greet(sibling)
    for j in range(1, ZS):
        greet(at_z(j))
    for j in range(1, YS):
        greet(at_y(j))
    for dx in range(1, NX):
        pl.semaphore_signal(barrier, inc=1, device_id={"chan": peer(dx)}, device_id_type=MESH)
    greetings = T + 2 + 1 + ZS - 1 + YS - 1 + NX - 1
    absent = jnp.where(x == 0, 1, 0) + jnp.where(me == 0, 1, 0) + jnp.where(me == NB - 1, 1, 0)

    stage[:, CP - 16 :, :] = jnp.zeros((T, 16, W), BF)
    def band_of(t):
        return lax.rem(me + x + NX * place_of(t), NB)

    def first_copy(t):
        rows = pl.ds(0, W)
        return to_band(stage.at[t, rows, :], recv.at[rows, cols(t)], f_s.at[t], f_r.at[t], band_of(t))

    def rest_copy(t):
        rows = pl.ds(W, CP - W)
        return to_band(stage.at[t, rows, :], recv.at[rows, cols(t)], a_s.at[t], a_r.at[t], band_of(t))

    def grid_copy(t):
        return to_band(stage.at[t], recv.at[:, cols(t)], a_s.at[t], a_r.at[t], band_of(t))

    def over_slots(lo, hi, body):
        def one(t, _):
            pl.when(x + place_of(t) != 0)(lambda: body(t))
            return 0

        lax.fori_loop(lo, hi, one, 0)

    for i, (a, b) in enumerate(steps):
        load_grid[i].wait()

        def by_block(k, _, i=i, n=b - a):
            blocks[k, 0:n, :] = flat_last[:, cols(k)] if i == 3 else flat[i % 2, :, cols(k)]
            return 0

        lax.fori_loop(0, NB, by_block, 0, unroll=4)
        if i == 0:
            load_grid[2].start()

        def to_stage(t, _, a=a, b=b):
            stage[t, a:b, :] = blocks[order[0, band_of(t)], 0 : b - a, :]
            return 0

        lax.fori_loop(0, T, to_stage, 0, unroll=2)
        if i == 0:
            pl.semaphore_wait(barrier, greetings - absent)
            over_slots(0, FIRST, lambda t: first_copy(t).start())
    over_slots(0, FIRST, lambda t: rest_copy(t).start())
    over_slots(FIRST, T - LATE, lambda t: grid_copy(t).start())
    load_mi.start()
    load_ce.start()

    @pl.when(x == 0)
    def _():
        recv[:, OWN * W : (OWN + 1) * W] = stage[OWN]

    load_wemb.wait()
    we_all[mine, CP - W : CP] = jnp.zeros((W, W), BF)
    we_all[mine, :C_IN] = wtmp[...].astype(F32).T.astype(BF)
    load_og.wait()
    load_wn.wait()
    wr_all[:, mine] = wn[mine, :]

    def early(dx):
        p = peer(dx)
        return (
            to_chan(we_all.at[mine, :], we_all.at[mine, :], x_s.at[0, dx], x_r.at[0, dx], p),
            to_chan(og_all.at[:, mine], og_all.at[:, mine], x_s.at[1, dx], x_r.at[1, dx], p),
            to_chan(wn.at[rows_of(p), :], wr_all.at[:, mine], x_s.at[2, dx], x_r.at[2, dx], p),
        )

    for dx in range(1, NX):
        for c in early(dx):
            c.start()

    def sum_cells(coef, pairs, count, hits):
        wide[0 : pairs * W, :] = coef[...].astype(F32)
        pick = jnp.where(hits, 1.0, 0.0).astype(BF)

        def one(i, _):
            line = wide[pl.ds(i, pairs, stride=W), :].astype(BF)
            cells[pl.ds(i, count, stride=W), :] = dot(pick, line)
            return 0

        lax.fori_loop(0, W, one, 0, unroll=4)

    def cell_ids(pairs):
        cell = lax.broadcasted_iota(jnp.int32, (CELLS, pairs), 0)
        return lax.shift_right_logical(cell, 4), lax.bitwise_and(cell, T - 1)

    load_ce.wait()
    cell = lax.broadcasted_iota(jnp.int32, (CELLS + LATE_CELLS, EP), 0)
    tail = cell - CELLS
    own_group = cell < CELLS
    cell_m = jnp.where(own_group, lax.shift_right_logical(cell, 4), lax.shift_right_arithmetic(tail, 3))
    cell_t = jnp.where(own_group, lax.bitwise_and(cell, T - 1), T - LATE + lax.bitwise_and(tail, LATE - 1))
    cell_x = jnp.where(own_group, x, lax.bitwise_and(lax.shift_right_arithmetic(tail, 1), NX - 1))
    cell_slot = lax.bitwise_and(me - cell_x - NX * place_of(cell_t) + 2 * NB, NB - 1)
    sum_cells(ce, EP, CELLS + LATE_CELLS, (edest[...] == cell_m) & (eslot[...] == cell_slot))

    load_cp.start()

    def enc_cells(t, _):
        for m in range(MB):
            a_enc[m * W : (m + 1) * W, cols(t)] = cells[rows_of(m * T + t), :].astype(BF)
        return 0

    lax.fori_loop(0, T, enc_cells, 0)

    def late_cells(t, _):
        for m in range(MB):
            a_late[m * W : (m + 1) * W, cols(t)] = cells[rows_of(CELLS + m * NX * LATE + t), :].astype(BF)
        return 0

    lax.fori_loop(0, NX * LATE, late_cells, 0)

    load_cp.wait()
    cell_m, cell_s = cell_ids(PP)
    sum_cells(cp, PP, CELLS, (pdest[...] == cell_m) & (psrc[...] == cell_s))

    def proc_cells(s, _):
        for m in range(MB):
            block = cells[rows_of(m * T + s), :]
            a_proc[m * W : (m + 1) * W, cols(s)] = block.astype(BF)
            at_proc[rows_of(s), m * W : (m + 1) * W] = block.T.astype(BF)
        return 0

    lax.fori_loop(0, 3 * MB, proc_cells, 0)

    for dx in range(1, NX):
        for c in early(dx):
            c.wait_recv()
    gh[...] = lax.dot_general(og_all[...], wr_all[...], (((1,), (1,)), ((), ())), preferred_element_type=F32)

    def sent_first(t):
        first_copy(t).wait_send()
        rest_copy(t).wait_send()

    over_slots(0, FIRST, sent_first)
    over_slots(FIRST, T - LATE, lambda t: grid_copy(t).wait_send())
    over_slots(T - LATE, T, lambda t: grid_copy(t).start())

    def dot_nt(a, b):
        return lax.dot_general(a, b, (((1,), (1,)), ((), ())), preferred_element_type=F32)

    enc_sum[...] = jnp.zeros((MR, LAT), F32)

    def embed(u):
        here = pl.ds(al(u * 2 * W, 2 * W), 2 * W)
        pre = dot(we_all[...], recv[:, here])
        sig = jax.nn.sigmoid(pre)
        slope[:, here] = slope_of(pre, sig)
        return (pre * sig).astype(BF), here

    def embed_sum(u, _):
        latent, here = embed(u)
        enc_sum[...] += dot_nt(a_enc[:, here], latent)
        return 0

    def first_slots(u, _):
        def arrive(t):
            first_copy(t).wait_recv()
            rest_copy(t).wait_recv()

        over_slots(2 * u, 2 * u + 2, arrive)
        return embed_sum(u, 0)

    def other_slots(u, _):
        over_slots(2 * u, 2 * u + 2, lambda t: grid_copy(t).wait_recv())
        return embed_sum(u, 0)

    lax.fori_loop(0, FIRST // 2, first_slots, 0)
    lax.fori_loop(FIRST // 2, (T - LATE) // 2, other_slots, 0)

    half = lax.div(x, 2)
    away = 1 - half
    twin = x + 1 - 2 * lax.rem(x, 2)
    far = (2 * away, 2 * away + 1)

    def two(h):
        return pl.ds(al(h * 2 * W, 2 * W), 2 * W)

    def enc_copy(c):
        return to_chan(part.at[:, cols(c)], rs1.at[x], c_s.at[0, c], c_r.at[0, x], c)

    part[:, two(away)] = enc_sum[:, two(away)].astype(BF)
    for c in far:
        enc_copy(c).start()
    part[:, cols(twin)] = enc_sum[:, cols(twin)].astype(BF)
    enc_copy(twin).start()

    def late_copy(v, c):
        return to_chan(lat_out.at[v, rows_of(c), :], lat_in.at[x, v], l_s.at[v, c], l_r.at[v, x], c)

    for v in range(LATE // 2):
        t = T - LATE + 2 * v
        over_slots(t, t + 2, lambda t: grid_copy(t).wait_recv())
        lat_out[v] = embed(t // 2)[0]
        for c in (*far, twin):
            late_copy(v, c).start()
    load_mi.wait()

    def late_sum(c):
        out = jnp.zeros((MR, W), F32)
        for v in range(LATE // 2):
            here = pl.ds(al((c * LATE + 2 * v) * W, 2 * W), 2 * W)
            out = out + dot_nt(a_late[:, here], lat_in[c, v])
        return out

    lat_in[x] = lat_out[:, mine, :]
    enc_pre = enc_sum[:, mine] + late_sum(x)
    for dx in range(1, NX):
        p = peer(dx)
        to_chan(part.at[:, cols(p)], rs1.at[p], c_s.at[0, p], c_r.at[0, p], p).wait_recv()
        enc_pre = enc_pre + rs1[p].astype(F32)
    for c in (twin, *far):
        for v in range(LATE // 2):
            to_chan(lat_out.at[v, rows_of(c), :], lat_in.at[c, v], l_s.at[v, c], l_r.at[v, c], c).wait_recv()
        enc_pre = enc_pre + late_sum(c)
    enc_sig = jax.nn.sigmoid(enc_pre)
    mesh_one = (mi[...].astype(F32) + enc_pre * enc_sig).astype(BF)
    enc_slope = slope_of(enc_pre, enc_sig)
    enc_slope_f[...] = enc_slope

    ext[MR : 2 * MR, :] = mesh_one
    own_ext = ext.at[MR : 2 * MR, :]
    halo_up = to_band(own_ext, ext.at[0:MR, :], h_s.at[0], h_r.at[0], high)
    halo_down = to_band(own_ext, ext.at[2 * MR : 3 * MR, :], h_s.at[1], h_r.at[1], low)
    pl.when(has_high)(halo_up.start)
    pl.when(has_low)(halo_down.start)
    mid[...] = dot(a_proc[:, MR : 2 * MR], mesh_one)

    @pl.when(me == 0)
    def _():
        ext[0:MR, :] = jnp.zeros((MR, W), BF)

    @pl.when(me == NB - 1)
    def _():
        ext[2 * MR : 3 * MR, :] = jnp.zeros((MR, W), BF)

    pl.when(has_low)(halo_up.wait_recv)
    pl.when(has_high)(halo_down.wait_recv)
    proc_pre = (
        mid[...]
        + dot(a_proc[:, 0:MR], ext[0:MR, :])
        + dot(a_proc[:, 2 * MR : 3 * MR], ext[2 * MR : 3 * MR, :])
    )
    proc_sig = jax.nn.sigmoid(proc_pre)
    hidden = (proc_pre * proc_sig).astype(BF)
    hid_all[:, mine] = hidden

    def hid_copy(c):
        return to_chan(hid_all.at[:, mine], hid_all.at[:, mine], c_s.at[1, c], c_r.at[1, x], c)

    grad_proc = (gh[...] * slope_of(proc_pre, proc_sig)).astype(BF)

    hb_out[0] = dot(at_proc[0:MR, :], grad_proc).astype(BF)
    back_down = to_band(hb_out.at[0], hb_in.at[0], b_s.at[0], b_r.at[0], low)
    pl.when(has_low)(back_down.start)
    hb_out[1] = dot(at_proc[2 * MR : 3 * MR, :], grad_proc).astype(BF)
    back_up = to_band(hb_out.at[1], hb_in.at[1], b_s.at[1], b_r.at[1], high)
    pl.when(has_high)(back_up.start)
    mid[...] = dot(at_proc[MR : 2 * MR, :], grad_proc) + og_all[:, mine].astype(F32)

    gn_out[...] = dot(hidden.astype(F32).T.astype(BF), og_all[...])
    gn_in[mine, :] = gn_out[:, mine]

    def gn_copy(c):
        return to_chan(gn_out.at[:, cols(c)], gn_in.at[mine, :], c_s.at[2, c], c_r.at[2, x], c)

    for dx in range(1, NX):
        gn_copy(peer(dx)).start()

    @pl.when(me == NB - 1)
    def _():
        hb_in[0] = jnp.zeros((MR, W), BF)

    @pl.when(me == 0)
    def _():
        hb_in[1] = jnp.zeros((MR, W), BF)

    pl.when(has_high)(back_down.wait_recv)
    pl.when(has_low)(back_up.wait_recv)
    total = mid[...] + hb_in[0].astype(F32) + hb_in[1].astype(F32)
    mg[...] = total
    save_grad = pltpu.make_async_copy(mg, mesh_grad, lsem.at[1])
    save_grad.start()
    ge_all[mine, :] = (total * enc_slope_f[...]).T.astype(BF)

    def ge_copy(c):
        return to_chan(ge_all.at[mine, :], ge_all.at[mine, :], c_s.at[3, c], c_r.at[3, x], c)

    def ge_wait(c):
        to_chan(ge_all.at[rows_of(c), :], ge_all.at[rows_of(c), :], c_s.at[3, c], c_r.at[3, c], c).wait_recv()

    for c in (twin, *far):
        ge_copy(c).start()

    keep = pl.ds(al(core * 256, 256), 256)
    give = pl.ds(al((1 - core) * 256, 256), 256)
    pieces = (pieces_e, pieces_n)
    landed = (landed_e, landed_n)
    result = (fin_e, fin_n)
    other = (fin_e2, fin_n2)

    def z_of(j):
        return lax.rem(z_here + j, ZS)

    def sum_z(k, j):
        return to_band(pieces[k].at[z_of(j)], landed[k].at[z_here], u_s.at[k, j], u_r.at[k, j], at_z(j))

    def sum_y(k, j):
        return to_band(by_y.at[k, y_here], by_y.at[k, y_here], v_s.at[k, j], v_r.at[k, j], at_y(j))

    def back_z(k, j):
        return to_band(result[k].at[z_here], result[k].at[z_here], u_s.at[2 + k, j], u_r.at[2 + k, j], at_z(j))

    def start_z(k):
        for j in range(1, ZS):
            sum_z(k, j).start()
        landed[k][z_here] = pieces[k][z_here]

    def start_y(k):
        for j in range(1, ZS):
            sum_z(k, j).wait_recv()
        by_y[k, y_here] = jnp.sum(landed[k][...].astype(F32), axis=0)
        for j in range(1, YS):
            sum_y(k, j).start()

    def start_back(k):
        for j in range(1, YS):
            y = lax.rem(y_here - j + YS, YS)
            to_band(by_y.at[k, y], by_y.at[k, y], v_s.at[k, j], v_r.at[k, j], at_y(j)).wait_recv()
        result[k][z_here] = jnp.sum(by_y[k], axis=0).astype(result[k].dtype)
        for j in range(1, ZS):
            back_z(k, j).start()

    def swap_back(k):
        for j in range(1, ZS):
            z = lax.rem(z_here - j + ZS, ZS)
            to_band(result[k].at[z], result[k].at[z], u_s.at[2 + k, j], u_r.at[2 + k, j], at_z(j)).wait_recv()
        copy = to_band(result[k], other[k], t_s.at[2 + k], t_r.at[2 + k], sibling)
        copy.start()
        return copy

    for dx in range(1, NX):
        p = peer(dx)
        prow = pl.ds(al(p * W, W), W)
        to_chan(gn_out.at[:, cols(p)], gn_in.at[prow, :], c_s.at[2, p], c_r.at[2, p], p).wait_recv()
    node_swap = to_band(gn_in.at[give, :], node_in, t_s.at[0], t_r.at[0], sibling)
    node_swap.start()
    node_swap.wait_recv()
    pieces_n[...] = (gn_in[keep, :] + node_in[...]).reshape(ZS, ZR, W)
    start_z(1)

    gemb_f = enc_sum.at[0:CP, 0 : 2 * W]

    def back(h):
        def piece(t, _):
            here = pl.ds(al(t * 512, 512), 512)
            msg = dot(ge_all[two(h), :], a_enc[:, here])
            gp[:, here] = (msg * slope[two(h), here]).astype(BF)
            return 0

        lax.fori_loop(0, ER // 512, piece, 0)
        gemb_f[...] = dot_nt(recv[...], gp[...])

    keep_rows = pl.ds(al(core * HALF, 16), HALF)
    give_rows = pl.ds(al((1 - core) * HALF, 16), HALF)

    def half_copy(k):
        return to_band(half_out.at[k], half_in.at[k], h_s.at[2 + k], h_r.at[2 + k], sibling)

    def ge2_copy(c):
        return to_chan(gemb_out.at[:, cols(c)], rs2.at[x], c_s.at[4, c], c_r.at[4, x], c)

    ge_wait(twin)
    back(half)
    half_out[0] = gemb_f[give_rows, :]
    half_copy(0).start()
    half_f[0] = gemb_f[keep_rows, :]
    start_y(1)
    for c in far:
        ge_wait(c)
    back(away)
    half_out[1] = gemb_f[give_rows, :]
    half_copy(1).start()
    half_f[1] = gemb_f[keep_rows, :]
    half_copy(0).wait_recv()
    half_f[0] = half_f[0] + half_in[0]
    gemb_out[:, two(half)] = half_f[0].astype(BF)
    ge2_copy(twin).start()
    half_copy(1).wait_recv()
    gemb_out[:, two(away)] = (half_f[1] + half_in[1]).astype(BF)
    for c in far:
        ge2_copy(c).start()
    start_back(1)
    total = half_f[0, :, pl.ds(al(lax.rem(x, 2) * W, W), W)]
    for dx in range(1, NX):
        p = peer(dx)
        to_chan(gemb_out.at[:, cols(p)], rs2.at[p], c_s.at[4, p], c_r.at[4, p], p).wait_recv()
        total = total + rs2[p].astype(F32)
    padded = jnp.concatenate([total, jnp.zeros((ZS * ZR - HALF, W), F32)], axis=0)
    pieces_e[...] = padded.astype(BF).reshape(ZS, ZR, W)
    start_z(0)
    for dx in range(1, NX):
        hid_copy(peer(dx)).start()
    node_back = swap_back(1)
    start_y(0)
    start_back(0)

    for dx in range(1, NX):
        p = peer(dx)
        to_chan(hid_all.at[:, cols(p)], hid_all.at[:, cols(p)], c_s.at[1, p], c_r.at[1, p], p).wait_recv()
    mo[...] = (ext[MR : 2 * MR, :].astype(F32) + dot(hid_all[...], wn[...])).astype(BF)
    save_out = pltpu.make_async_copy(mo, mesh_out, lsem.at[2])
    save_out.start()
    node_back.wait_recv()
    node_saves = [pltpu.make_async_copy(fin_n, node_out, lsem.at[3]), pltpu.make_async_copy(fin_n2, node2_out, lsem.at[4])]
    for c in node_saves:
        c.start()
    last_back = swap_back(0)
    last_save = pltpu.make_async_copy(fin_e, fin_out, lsem.at[5])
    last_save.start()
    last_back.wait_recv()
    last_save2 = pltpu.make_async_copy(fin_e2, fin2_out, lsem.at[6])
    last_save2.start()
    saves = (*node_saves, last_save, last_save2)

    over_slots(T - LATE, T, lambda t: grid_copy(t).wait_send())
    for dx in range(1, NX):
        p = peer(dx)
        for c in early(dx):
            c.wait_send()
        for v in range(LATE // 2):
            late_copy(v, p).wait_send()
        for f in (enc_copy, hid_copy, gn_copy, ge_copy, ge2_copy):
            f(p).wait_send()
    pl.when(has_high)(halo_up.wait_send)
    pl.when(has_low)(halo_down.wait_send)
    pl.when(has_low)(back_down.wait_send)
    pl.when(has_high)(back_up.wait_send)
    for k in range(2):
        half_copy(k).wait_send()
    for c in (node_swap, node_back, last_back):
        c.wait_send()

    for k in range(2):
        for j in range(1, ZS):
            sum_z(k, j).wait_send()
            back_z(k, j).wait_send()
        for j in range(1, YS):
            sum_y(k, j).wait_send()
    save_grad.wait()
    save_out.wait()
    for c in saves:
        c.wait()


def on_device(
    grid_in, w_embed, send_order, enc_coef, enc_slot, enc_dest, mesh_in, proc_coef, proc_src, proc_dest, w_node, out_grad
):
    smem = pl.BlockSpec(memory_space=pltpu.SMEM)
    hbm = pl.BlockSpec(memory_space=pl.ANY)
    vmem = pl.BlockSpec(memory_space=pltpu.VMEM)
    V = pltpu.VMEM
    dma = pltpu.SemaphoreType.DMA
    piece = jax.ShapeDtypeStruct((ZS, ZR, W), F32)
    piece_bf = jax.ShapeDtypeStruct((ZS, ZR, W), BF)
    parts = pl.pallas_call(
        kernel,
        out_shape=(
            jax.ShapeDtypeStruct((MR, W), BF),
            jax.ShapeDtypeStruct((MR, W), F32),
            piece_bf, piece_bf, piece, piece,
        ),
        in_specs=[smem] + [vmem] * 4 + [hbm] * 7,
        out_specs=(hbm,) * 6,
        scratch_shapes=[
            V((2, W, NB * W), BF),
            V((C_IN - 3 * W, NB * W), BF),
            V((NB, W, W), BF),
            V((T, CP, W), BF),
            V((CP, ER), BF),
            V((LAT, CP), BF),
            V((C_IN, W), BF),
            V((MR, LAT), BF),
            V((LAT, W), BF),
            V((W, LAT), BF),
            V((MR, W), BF),
            V((EP * W, W), BF),
            V((EP * W, W), F32),
            V(((CELLS + LATE_CELLS) * W, W), F32),
            V((MR, ER), BF),
            V((MR, NX * LATE * W), BF),
            V((MR, 3 * MR), BF),
            V((3 * MR, MR), BF),
            V((MR, W), F32),
            V((LAT, ER), F32),
            V((MR, LAT), BF),
            V((MR, LAT), F32),
            V((MR, W), F32),
            V((NX, MR, W), BF),
            V((LATE // 2, LAT, 2 * W), BF),
            V((NX, LATE // 2, W, 2 * W), BF),
            V((3 * MR, W), BF),
            V((MR, LAT), BF),
            V((2, MR, W), BF),
            V((2, MR, W), BF),
            V((MR, W), F32),
            V((W, LAT), F32),
            V((LAT, W), F32),
            V((LAT, MR), BF),
            V((2 * W, ER), BF),
            V((2, HALF, 2 * W), F32),
            V((2, HALF, 2 * W), F32),
            V((2, HALF, 2 * W), F32),
            V((HALF, LAT), BF),
            V((NX, HALF, W), BF),
            V((256, W), F32),
            V((ZS, ZR, W), BF),
            V((ZS, ZR, W), F32),
            V((ZS, ZR, W), BF),
            V((ZS, ZR, W), F32),
            V((2, YS, ZR, W), F32),
            V((ZS, ZR, W), BF),
            V((ZS, ZR, W), BF),
            V((ZS, ZR, W), F32),
            V((ZS, ZR, W), F32),
            V((MR, W), BF),
            V((MR, W), F32),
            dma((7,)),
            dma((4,)),
            dma((FIRST,)), dma((FIRST,)),
            dma((T,)), dma((T,)),
            dma((3, NX)), dma((3, NX)),
            dma((4,)), dma((4,)),
            dma((2,)), dma((2,)),
            dma((5, NX)), dma((5, NX)),
            dma((4,)), dma((4,)),
            dma((4, ZS)), dma((4, ZS)),
            dma((2, YS)), dma((2, YS)),
            dma((LATE // 2, NX)), dma((LATE // 2, NX)),
        ],
        compiler_params=pltpu.CompilerParams(
            collective_id=0, has_side_effects=True, vmem_limit_bytes=60 << 20
        ),
    )(
        send_order, enc_slot, enc_dest, proc_src, proc_dest, grid_in.T,
        w_embed, enc_coef.reshape(EP * W, W), mesh_in,
        proc_coef.reshape(PP * W, W), w_node, out_grad,
    )
    return pl.pallas_call(
        finish,
        out_shape=(
            jax.ShapeDtypeStruct((MR, W), BF),
            jax.ShapeDtypeStruct((MR, W), F32),
            jax.ShapeDtypeStruct((C_IN, W), F32),
            jax.ShapeDtypeStruct((LAT, W), F32),
        ),
        in_specs=[vmem] * 6,
        out_specs=(vmem,) * 4,
        compiler_params=pltpu.CompilerParams(vmem_limit_bytes=60 << 20),
    )(*parts)


def solution(mesh):
    return jax.shard_map(
        on_device,
        mesh=mesh,
        in_specs=(
            P("band", None),
            P(None, "chan"),
            P("band", None),
            P("band", None, None),
            P("band", None),
            P("band", None),
            P("band", "chan"),
            P("band", None, None),
            P("band", None),
            P("band", None),
            P(None, "chan"),
            P("band", "chan"),
        ),
        out_specs=(P("band", "chan"), P("band", "chan"), P(None, "chan"), P(None, "chan")),
        check_vma=False,
    )
```

```python
import jax
import jax.numpy as jnp
from jax import lax
from jax.experimental import pallas as pl
from jax.experimental.pallas import tpu as pltpu
from jax.sharding import PartitionSpec as P

MESH = pl.DeviceIdType.MESH
F32 = jnp.float32
BF = jnp.bfloat16
NB = 64
NX = 4
C_IN = 474
CP = 480
LAT = 512
W = 128
T = NB // NX
EP = 96
PP = 48
MB = 5
MR = MB * W
ER = T * W
CELLS = MB * T
LATE = 2
LATE_CELLS = MB * NX * LATE
OWN = 1
FIRST = 4
ZS = 8
YS = 4
ZR = 32
HALF = CP // 2


def place_of(t):
    return (3 * t + 13) & (T - 1)


def dot(a, b):
    return jnp.dot(a, b, preferred_element_type=F32)


def slope_of(v, s):
    return s * (1.0 + v * (1.0 - s))


def al(v, m):
    return pl.multiple_of(v, m)


def finish(out_in, grad_in, fin, fin2, node_fin, node_fin2, mesh_out, mesh_grad, gemb, gnode):
    core = lax.rem(lax.axis_index("band"), 2)
    mesh_out[...] = out_in[...]
    mesh_grad[...] = grad_in[...]
    gnode[pl.ds(al(core * 256, 256), 256), :] = node_fin[...].reshape(256, W)
    gnode[pl.ds(al((1 - core) * 256, 256), 256), :] = node_fin2[...].reshape(256, W)

    def write(low, high):
        gemb[0:HALF, :] = low[...].reshape(256, W)[:HALF].astype(F32)
        gemb[HALF:C_IN, :] = high[...].reshape(256, W)[: C_IN - HALF].astype(F32)

    @pl.when(core == 0)
    def _():
        write(fin, fin2)

    @pl.when(core == 1)
    def _():
        write(fin2, fin)


def kernel(
    order, eslot, edest, psrc, pdest, grid, wemb, ecoef, meshin, pcoef, wnode, ograd,
    mesh_out, mesh_grad, fin_out, fin2_out, node_out, node2_out,
    flat, flat_last, blocks, stage, recv, we_all, wtmp, og_all, wn, wr_all, mi, ce,
    wide, cells, a_enc, a_late, a_proc, at_proc, gh, slope,
    part, enc_sum, enc_slope_f, rs1, lat_out, lat_in, ext, hid_all, hb_out, hb_in, mid, gn_out, gn_in, ge_all, gp,
    half_f, half_out, half_in, gemb_out, rs2, node_in, pieces_e, pieces_n, landed_e, landed_n, by_y, fin_e, fin_e2, fin_n, fin_n2, mo, mg,
    lsem, g_s, f_s, f_r, a_s, a_r, x_s, x_r, h_s, h_r, b_s, b_r, c_s, c_r, t_s, t_r, u_s, u_r, v_s, v_r, l_s, l_r,
):
    me = lax.axis_index("band")
    x = lax.axis_index("chan")
    core = lax.rem(me, 2)
    chip = lax.div(me, 2)
    mine = pl.ds(al(x * W, W), W)

    def to_band(src, dst, ss, rs, band):
        return pltpu.make_async_remote_copy(src, dst, ss, rs, device_id={"band": band}, device_id_type=MESH)

    def to_chan(src, dst, ss, rs, chan):
        return pltpu.make_async_remote_copy(src, dst, ss, rs, device_id={"chan": chan}, device_id_type=MESH)

    def peer(dx):
        return lax.rem(x + dx, NX)

    def cols(c):
        return pl.ds(al(c * W, W), W)

    def rows_of(c):
        return pl.ds(al(c * W, W), W)

    barrier = pltpu.get_barrier_semaphore()

    def greet(band):
        pl.semaphore_signal(barrier, inc=1, device_id={"band": band}, device_id_type=MESH)

    z_here = lax.div(me, 8)
    y_here = lax.rem(chip, YS)
    has_low = me > 0
    has_high = me < NB - 1
    low = lax.rem(me + NB - 1, NB)
    high = lax.rem(me + 1, NB)
    sibling = me + 1 - 2 * core

    def at_z(j):
        return lax.rem(me + 8 * j, NB)

    def at_y(j):
        return z_here * 8 + lax.rem(y_here + j, YS) * 2 + core

    def greet_source(t, _):
        @pl.when(x + t != 0)
        def _():
            greet(lax.rem(me - x - NX * t + 2 * NB, NB))

        return 0

    lax.fori_loop(0, T, greet_source, 0)
    pl.when(has_low)(lambda: greet(low))
    pl.when(has_high)(lambda: greet(high))
    greet(sibling)
    for j in range(1, ZS):
        greet(at_z(j))
    for j in range(1, YS):
        greet(at_y(j))
    for dx in range(1, NX):
        pl.semaphore_signal(barrier, inc=1, device_id={"chan": peer(dx)}, device_id_type=MESH)
    greetings = T + 2 + 1 + ZS - 1 + YS - 1 + NX - 1
    absent = jnp.where(x == 0, 1, 0) + jnp.where(me == 0, 1, 0) + jnp.where(me == NB - 1, 1, 0)

    steps = ((0, 128), (128, 256), (256, 384), (384, C_IN))
    load_grid = [
        pltpu.make_async_copy(grid.at[a:b, :], flat_last if i == 3 else flat.at[i % 2], g_s.at[i])
        for i, (a, b) in enumerate(steps)
    ]
    for i in (0, 1, 3):
        load_grid[i].start()
    load_wemb = pltpu.make_async_copy(wemb, wtmp, lsem.at[1])
    load_og = pltpu.make_async_copy(ograd, og_all.at[:, mine], lsem.at[2])
    load_wn = pltpu.make_async_copy(wnode, wn, lsem.at[3])
    load_mi = pltpu.make_async_copy(meshin, mi, lsem.at[4])
    load_ce = pltpu.make_async_copy(ecoef, ce, lsem.at[5])
    cp = ce.at[0 : PP * W, :]
    load_cp = pltpu.make_async_copy(pcoef, cp, lsem.at[6])
    load_wemb.start()
    load_og.start()
    load_wn.start()

    stage[:, CP - 16 :, :] = jnp.zeros((T, 16, W), BF)
    def band_of(t):
        return lax.rem(me + x + NX * place_of(t), NB)

    def first_copy(t):
        rows = pl.ds(0, W)
        return to_band(stage.at[t, rows, :], recv.at[rows, cols(t)], f_s.at[t], f_r.at[t], band_of(t))

    def rest_copy(t):
        rows = pl.ds(W, CP - W)
        return to_band(stage.at[t, rows, :], recv.at[rows, cols(t)], a_s.at[t], a_r.at[t], band_of(t))

    def grid_copy(t):
        return to_band(stage.at[t], recv.at[:, cols(t)], a_s.at[t], a_r.at[t], band_of(t))

    def over_slots(lo, hi, body):
        def one(t, _):
            pl.when(x + place_of(t) != 0)(lambda: body(t))
            return 0

        lax.fori_loop(lo, hi, one, 0)

    for i, (a, b) in enumerate(steps):
        load_grid[i].wait()

        def by_block(k, _, i=i, n=b - a):
            blocks[k, 0:n, :] = flat_last[:, cols(k)] if i == 3 else flat[i % 2, :, cols(k)]
            return 0

        lax.fori_loop(0, NB, by_block, 0, unroll=4)
        if i == 0:
            load_grid[2].start()

        def to_stage(t, _, a=a, b=b):
            stage[t, a:b, :] = blocks[order[0, band_of(t)], 0 : b - a, :]
            return 0

        lax.fori_loop(0, T, to_stage, 0, unroll=2)
        if i == 0:
            pl.semaphore_wait(barrier, greetings - absent)
            over_slots(0, FIRST, lambda t: first_copy(t).start())
    over_slots(0, FIRST, lambda t: rest_copy(t).start())
    over_slots(FIRST, T - LATE, lambda t: grid_copy(t).start())
    load_mi.start()
    load_ce.start()

    @pl.when(x == 0)
    def _():
        recv[:, OWN * W : (OWN + 1) * W] = stage[OWN]

    load_wemb.wait()
    we_all[mine, CP - W : CP] = jnp.zeros((W, W), BF)
    we_all[mine, :C_IN] = wtmp[...].astype(F32).T.astype(BF)
    load_og.wait()
    load_wn.wait()
    wr_all[:, mine] = wn[mine, :]

    def early(dx):
        p = peer(dx)
        return (
            to_chan(we_all.at[mine, :], we_all.at[mine, :], x_s.at[0, dx], x_r.at[0, dx], p),
            to_chan(og_all.at[:, mine], og_all.at[:, mine], x_s.at[1, dx], x_r.at[1, dx], p),
            to_chan(wn.at[rows_of(p), :], wr_all.at[:, mine], x_s.at[2, dx], x_r.at[2, dx], p),
        )

    for dx in range(1, NX):
        for c in early(dx):
            c.start()

    def sum_cells(coef, pairs, count, hits):
        wide[0 : pairs * W, :] = coef[...].astype(F32)
        pick = jnp.where(hits, 1.0, 0.0).astype(BF)

        def one(i, _):
            line = wide[pl.ds(i, pairs, stride=W), :].astype(BF)
            cells[pl.ds(i, count, stride=W), :] = dot(pick, line)
            return 0

        lax.fori_loop(0, W, one, 0, unroll=4)

    def cell_ids(pairs):
        cell = lax.broadcasted_iota(jnp.int32, (CELLS, pairs), 0)
        return lax.shift_right_logical(cell, 4), lax.bitwise_and(cell, T - 1)

    load_ce.wait()
    cell = lax.broadcasted_iota(jnp.int32, (CELLS + LATE_CELLS, EP), 0)
    tail = cell - CELLS
    own_group = cell < CELLS
    cell_m = jnp.where(own_group, lax.shift_right_logical(cell, 4), lax.shift_right_arithmetic(tail, 3))
    cell_t = jnp.where(own_group, lax.bitwise_and(cell, T - 1), T - LATE + lax.bitwise_and(tail, LATE - 1))
    cell_x = jnp.where(own_group, x, lax.bitwise_and(lax.shift_right_arithmetic(tail, 1), NX - 1))
    cell_slot = lax.bitwise_and(me - cell_x - NX * place_of(cell_t) + 2 * NB, NB - 1)
    sum_cells(ce, EP, CELLS + LATE_CELLS, (edest[...] == cell_m) & (eslot[...] == cell_slot))

    load_cp.start()

    def enc_cells(t, _):
        for m in range(MB):
            a_enc[m * W : (m + 1) * W, cols(t)] = cells[rows_of(m * T + t), :].astype(BF)
        return 0

    lax.fori_loop(0, T, enc_cells, 0)

    def late_cells(t, _):
        for m in range(MB):
            a_late[m * W : (m + 1) * W, cols(t)] = cells[rows_of(CELLS + m * NX * LATE + t), :].astype(BF)
        return 0

    lax.fori_loop(0, NX * LATE, late_cells, 0)

    load_cp.wait()
    cell_m, cell_s = cell_ids(PP)
    sum_cells(cp, PP, CELLS, (pdest[...] == cell_m) & (psrc[...] == cell_s))

    def proc_cells(s, _):
        for m in range(MB):
            block = cells[rows_of(m * T + s), :]
            a_proc[m * W : (m + 1) * W, cols(s)] = block.astype(BF)
            at_proc[rows_of(s), m * W : (m + 1) * W] = block.T.astype(BF)
        return 0

    lax.fori_loop(0, 3 * MB, proc_cells, 0)

    for dx in range(1, NX):
        for c in early(dx):
            c.wait_recv()
    gh[...] = lax.dot_general(og_all[...], wr_all[...], (((1,), (1,)), ((), ())), preferred_element_type=F32)

    def sent_first(t):
        first_copy(t).wait_send()
        rest_copy(t).wait_send()

    over_slots(0, FIRST, sent_first)
    over_slots(FIRST, 8, lambda t: grid_copy(t).wait_send())
    over_slots(T - LATE, T, lambda t: grid_copy(t).start())
    over_slots(8, T - LATE, lambda t: grid_copy(t).wait_send())

    def dot_nt(a, b):
        return lax.dot_general(a, b, (((1,), (1,)), ((), ())), preferred_element_type=F32)

    enc_sum[...] = jnp.zeros((MR, LAT), F32)

    def embed(here):
        pre = dot(we_all[...], recv[:, here])
        sig = jax.nn.sigmoid(pre)
        slope[:, here] = slope_of(pre, sig)
        return (pre * sig).astype(BF)

    def embed_sum(u, _):
        here = pl.ds(al(u * 2 * W, 2 * W), 2 * W)
        latent = embed(here)
        enc_sum[...] += dot_nt(a_enc[:, here], latent)
        return 0

    def first_slots(u, _):
        def arrive(t):
            first_copy(t).wait_recv()
            rest_copy(t).wait_recv()

        over_slots(2 * u, 2 * u + 2, arrive)
        return embed_sum(u, 0)

    def other_slots(u, _):
        over_slots(2 * u, 2 * u + 2, lambda t: grid_copy(t).wait_recv())
        return embed_sum(u, 0)

    lax.fori_loop(0, FIRST // 2, first_slots, 0)
    lax.fori_loop(FIRST // 2, (T - LATE) // 2, other_slots, 0)

    half = lax.div(x, 2)
    away = 1 - half
    twin = x + 1 - 2 * lax.rem(x, 2)
    far = (2 * away, 2 * away + 1)

    def two(h):
        return pl.ds(al(h * 2 * W, 2 * W), 2 * W)

    def enc_copy(c):
        return to_chan(part.at[:, cols(c)], rs1.at[x], c_s.at[0, c], c_r.at[0, x], c)

    part[:, two(away)] = enc_sum[:, two(away)].astype(BF)
    for c in far:
        enc_copy(c).start()
    part[:, cols(twin)] = enc_sum[:, cols(twin)].astype(BF)
    enc_copy(twin).start()

    def late_copy(v, c):
        return to_chan(lat_out.at[v, rows_of(c), :], lat_in.at[x, v], l_s.at[v, c], l_r.at[v, x], c)

    for v in range(LATE):
        t = T - LATE + v
        grid_copy(t).wait_recv()
        lat_out[v] = embed(pl.ds(t * W, W))
        for c in (*far, twin):
            late_copy(v, c).start()
    load_mi.wait()

    def late_sum(c):
        out = jnp.zeros((MR, W), F32)
        for v in range(LATE):
            out = out + dot_nt(a_late[:, cols(c * LATE + v)], lat_in[c, v])
        return out

    lat_in[x] = lat_out[:, mine, :]
    enc_pre = enc_sum[:, mine] + late_sum(x)
    for dx in range(1, NX):
        p = peer(dx)
        to_chan(part.at[:, cols(p)], rs1.at[p], c_s.at[0, p], c_r.at[0, p], p).wait_recv()
        enc_pre = enc_pre + rs1[p].astype(F32)
    for c in (twin, *far):
        for v in range(LATE):
            to_chan(lat_out.at[v, rows_of(c), :], lat_in.at[c, v], l_s.at[v, c], l_r.at[v, c], c).wait_recv()
        enc_pre = enc_pre + late_sum(c)
    enc_sig = jax.nn.sigmoid(enc_pre)
    mesh_one = (mi[...].astype(F32) + enc_pre * enc_sig).astype(BF)
    enc_slope = slope_of(enc_pre, enc_sig)
    enc_slope_f[...] = enc_slope

    ext[MR : 2 * MR, :] = mesh_one
    own_ext = ext.at[MR : 2 * MR, :]
    halo_up = to_band(own_ext, ext.at[0:MR, :], h_s.at[0], h_r.at[0], high)
    halo_down = to_band(own_ext, ext.at[2 * MR : 3 * MR, :], h_s.at[1], h_r.at[1], low)
    pl.when(has_high)(halo_up.start)
    pl.when(has_low)(halo_down.start)
    mid[...] = dot(a_proc[:, MR : 2 * MR], mesh_one)

    @pl.when(me == 0)
    def _():
        ext[0:MR, :] = jnp.zeros((MR, W), BF)

    @pl.when(me == NB - 1)
    def _():
        ext[2 * MR : 3 * MR, :] = jnp.zeros((MR, W), BF)

    pl.when(has_low)(halo_up.wait_recv)
    mid[...] += dot(a_proc[:, 0:MR], ext[0:MR, :])
    pl.when(has_high)(halo_down.wait_recv)
    proc_pre = mid[...] + dot(a_proc[:, 2 * MR : 3 * MR], ext[2 * MR : 3 * MR, :])
    proc_sig = jax.nn.sigmoid(proc_pre)
    hidden = (proc_pre * proc_sig).astype(BF)
    hid_all[:, mine] = hidden

    def hid_copy(c):
        return to_chan(hid_all.at[:, mine], hid_all.at[:, mine], c_s.at[1, c], c_r.at[1, x], c)

    grad_proc = (gh[...] * slope_of(proc_pre, proc_sig)).astype(BF)

    hb_out[0] = dot(at_proc[0:MR, :], grad_proc).astype(BF)
    back_down = to_band(hb_out.at[0], hb_in.at[0], b_s.at[0], b_r.at[0], low)
    pl.when(has_low)(back_down.start)
    hb_out[1] = dot(at_proc[2 * MR : 3 * MR, :], grad_proc).astype(BF)
    back_up = to_band(hb_out.at[1], hb_in.at[1], b_s.at[1], b_r.at[1], high)
    pl.when(has_high)(back_up.start)
    mid[...] = dot(at_proc[MR : 2 * MR, :], grad_proc) + og_all[:, mine].astype(F32)

    gn_out[...] = dot(hidden.astype(F32).T.astype(BF), og_all[...])
    gn_in[mine, :] = gn_out[:, mine]

    def gn_copy(c):
        return to_chan(gn_out.at[:, cols(c)], gn_in.at[mine, :], c_s.at[2, c], c_r.at[2, x], c)

    for dx in range(1, NX):
        gn_copy(peer(dx)).start()

    @pl.when(me == NB - 1)
    def _():
        hb_in[0] = jnp.zeros((MR, W), BF)

    @pl.when(me == 0)
    def _():
        hb_in[1] = jnp.zeros((MR, W), BF)

    pl.when(has_high)(back_down.wait_recv)
    pl.when(has_low)(back_up.wait_recv)
    total = mid[...] + hb_in[0].astype(F32) + hb_in[1].astype(F32)
    mg[...] = total
    save_grad = pltpu.make_async_copy(mg, mesh_grad, lsem.at[1])
    save_grad.start()
    ge_all[mine, :] = (total * enc_slope_f[...]).T.astype(BF)

    def ge_copy(c):
        return to_chan(ge_all.at[mine, :], ge_all.at[mine, :], c_s.at[3, c], c_r.at[3, x], c)

    def ge_wait(c):
        to_chan(ge_all.at[rows_of(c), :], ge_all.at[rows_of(c), :], c_s.at[3, c], c_r.at[3, c], c).wait_recv()

    for c in (twin, *far):
        ge_copy(c).start()

    keep = pl.ds(al(core * 256, 256), 256)
    give = pl.ds(al((1 - core) * 256, 256), 256)
    pieces = (pieces_e, pieces_n)
    landed = (landed_e, landed_n)
    result = (fin_e, fin_n)
    other = (fin_e2, fin_n2)

    def z_of(j):
        return lax.rem(z_here + j, ZS)

    def sum_z(k, j):
        return to_band(pieces[k].at[z_of(j)], landed[k].at[z_here], u_s.at[k, j], u_r.at[k, j], at_z(j))

    def sum_y(k, j):
        return to_band(by_y.at[k, y_here], by_y.at[k, y_here], v_s.at[k, j], v_r.at[k, j], at_y(j))

    def back_z(k, j):
        return to_band(result[k].at[z_here], result[k].at[z_here], u_s.at[2 + k, j], u_r.at[2 + k, j], at_z(j))

    def start_z(k):
        for j in range(1, ZS):
            sum_z(k, j).start()
        landed[k][z_here] = pieces[k][z_here]

    def start_y(k):
        for j in range(1, ZS):
            sum_z(k, j).wait_recv()
        by_y[k, y_here] = jnp.sum(landed[k][...].astype(F32), axis=0)
        for j in range(1, YS):
            sum_y(k, j).start()

    def start_back(k):
        for j in range(1, YS):
            y = lax.rem(y_here - j + YS, YS)
            to_band(by_y.at[k, y], by_y.at[k, y], v_s.at[k, j], v_r.at[k, j], at_y(j)).wait_recv()
        result[k][z_here] = jnp.sum(by_y[k], axis=0).astype(result[k].dtype)
        for j in range(1, ZS):
            back_z(k, j).start()

    def swap_back(k):
        for j in range(1, ZS):
            z = lax.rem(z_here - j + ZS, ZS)
            to_band(result[k].at[z], result[k].at[z], u_s.at[2 + k, j], u_r.at[2 + k, j], at_z(j)).wait_recv()
        copy = to_band(result[k], other[k], t_s.at[2 + k], t_r.at[2 + k], sibling)
        copy.start()
        return copy

    for dx in range(1, NX):
        p = peer(dx)
        prow = pl.ds(al(p * W, W), W)
        to_chan(gn_out.at[:, cols(p)], gn_in.at[prow, :], c_s.at[2, p], c_r.at[2, p], p).wait_recv()
    node_swap = to_band(gn_in.at[give, :], node_in, t_s.at[0], t_r.at[0], sibling)
    node_swap.start()
    node_swap.wait_recv()
    pieces_n[...] = (gn_in[keep, :] + node_in[...]).reshape(ZS, ZR, W)
    start_z(1)

    gemb_f = enc_sum.at[0:CP, 0 : 2 * W]

    def back(h):
        def piece(t, _):
            here = pl.ds(al(t * 512, 512), 512)
            msg = dot(ge_all[two(h), :], a_enc[:, here])
            gp[:, here] = (msg * slope[two(h), here]).astype(BF)
            return 0

        lax.fori_loop(0, ER // 512, piece, 0)
        gemb_f[...] = dot_nt(recv[...], gp[...])

    keep_rows = pl.ds(al(core * HALF, 16), HALF)
    give_rows = pl.ds(al((1 - core) * HALF, 16), HALF)

    def half_copy(k):
        return to_band(half_out.at[k], half_in.at[k], h_s.at[2 + k], h_r.at[2 + k], sibling)

    def ge2_copy(c):
        return to_chan(gemb_out.at[:, cols(c)], rs2.at[x], c_s.at[4, c], c_r.at[4, x], c)

    ge_wait(twin)
    back(half)
    half_out[0] = gemb_f[give_rows, :]
    half_copy(0).start()
    half_f[0] = gemb_f[keep_rows, :]
    start_y(1)
    for c in far:
        ge_wait(c)
    back(away)
    half_out[1] = gemb_f[give_rows, :]
    half_copy(1).start()
    half_f[1] = gemb_f[keep_rows, :]
    half_copy(0).wait_recv()
    half_f[0] = half_f[0] + half_in[0]
    gemb_out[:, two(half)] = half_f[0].astype(BF)
    ge2_copy(twin).start()
    half_copy(1).wait_recv()
    gemb_out[:, two(away)] = (half_f[1] + half_in[1]).astype(BF)
    for c in far:
        ge2_copy(c).start()
    start_back(1)
    total = half_f[0, :, pl.ds(al(lax.rem(x, 2) * W, W), W)]
    for dx in range(1, NX):
        p = peer(dx)
        to_chan(gemb_out.at[:, cols(p)], rs2.at[p], c_s.at[4, p], c_r.at[4, p], p).wait_recv()
        total = total + rs2[p].astype(F32)
    padded = jnp.concatenate([total, jnp.zeros((ZS * ZR - HALF, W), F32)], axis=0)
    pieces_e[...] = padded.astype(BF).reshape(ZS, ZR, W)
    start_z(0)
    for dx in range(1, NX):
        hid_copy(peer(dx)).start()
    node_back = swap_back(1)
    start_y(0)
    start_back(0)

    for dx in range(1, NX):
        p = peer(dx)
        to_chan(hid_all.at[:, cols(p)], hid_all.at[:, cols(p)], c_s.at[1, p], c_r.at[1, p], p).wait_recv()
    mo[...] = (ext[MR : 2 * MR, :].astype(F32) + dot(hid_all[...], wn[...])).astype(BF)
    save_out = pltpu.make_async_copy(mo, mesh_out, lsem.at[2])
    save_out.start()
    node_back.wait_recv()
    node_saves = [pltpu.make_async_copy(fin_n, node_out, lsem.at[3]), pltpu.make_async_copy(fin_n2, node2_out, lsem.at[4])]
    for c in node_saves:
        c.start()
    last_back = swap_back(0)
    last_save = pltpu.make_async_copy(fin_e, fin_out, lsem.at[5])
    last_save.start()
    last_back.wait_recv()
    last_save2 = pltpu.make_async_copy(fin_e2, fin2_out, lsem.at[6])
    last_save2.start()
    saves = (*node_saves, last_save, last_save2)

    over_slots(T - LATE, T, lambda t: grid_copy(t).wait_send())
    for dx in range(1, NX):
        p = peer(dx)
        for c in early(dx):
            c.wait_send()
        for v in range(LATE):
            late_copy(v, p).wait_send()
        for f in (enc_copy, hid_copy, gn_copy, ge_copy, ge2_copy):
            f(p).wait_send()
    pl.when(has_high)(halo_up.wait_send)
    pl.when(has_low)(halo_down.wait_send)
    pl.when(has_low)(back_down.wait_send)
    pl.when(has_high)(back_up.wait_send)
    for k in range(2):
        half_copy(k).wait_send()
    for c in (node_swap, node_back, last_back):
        c.wait_send()

    for k in range(2):
        for j in range(1, ZS):
            sum_z(k, j).wait_send()
            back_z(k, j).wait_send()
        for j in range(1, YS):
            sum_y(k, j).wait_send()
    save_grad.wait()
    save_out.wait()
    for c in saves:
        c.wait()


def on_device(
    grid_in, w_embed, send_order, enc_coef, enc_slot, enc_dest, mesh_in, proc_coef, proc_src, proc_dest, w_node, out_grad
):
    smem = pl.BlockSpec(memory_space=pltpu.SMEM)
    hbm = pl.BlockSpec(memory_space=pl.ANY)
    vmem = pl.BlockSpec(memory_space=pltpu.VMEM)
    V = pltpu.VMEM
    dma = pltpu.SemaphoreType.DMA
    piece = jax.ShapeDtypeStruct((ZS, ZR, W), F32)
    piece_bf = jax.ShapeDtypeStruct((ZS, ZR, W), BF)
    parts = pl.pallas_call(
        kernel,
        out_shape=(
            jax.ShapeDtypeStruct((MR, W), BF),
            jax.ShapeDtypeStruct((MR, W), F32),
            piece_bf, piece_bf, piece, piece,
        ),
        in_specs=[smem] + [vmem] * 4 + [hbm] * 7,
        out_specs=(hbm,) * 6,
        scratch_shapes=[
            V((2, W, NB * W), BF),
            V((C_IN - 3 * W, NB * W), BF),
            V((NB, W, W), BF),
            V((T, CP, W), BF),
            V((CP, ER), BF),
            V((LAT, CP), BF),
            V((C_IN, W), BF),
            V((MR, LAT), BF),
            V((LAT, W), BF),
            V((W, LAT), BF),
            V((MR, W), BF),
            V((EP * W, W), BF),
            V((EP * W, W), F32),
            V(((CELLS + LATE_CELLS) * W, W), F32),
            V((MR, ER), BF),
            V((MR, NX * LATE * W), BF),
            V((MR, 3 * MR), BF),
            V((3 * MR, MR), BF),
            V((MR, W), F32),
            V((LAT, ER), F32),
            V((MR, LAT), BF),
            V((MR, LAT), F32),
            V((MR, W), F32),
            V((NX, MR, W), BF),
            V((LATE, LAT, W), BF),
            V((NX, LATE, W, W), BF),
            V((3 * MR, W), BF),
            V((MR, LAT), BF),
            V((2, MR, W), BF),
            V((2, MR, W), BF),
            V((MR, W), F32),
            V((W, LAT), F32),
            V((LAT, W), F32),
            V((LAT, MR), BF),
            V((2 * W, ER), BF),
            V((2, HALF, 2 * W), F32),
            V((2, HALF, 2 * W), F32),
            V((2, HALF, 2 * W), F32),
            V((HALF, LAT), BF),
            V((NX, HALF, W), BF),
            V((256, W), F32),
            V((ZS, ZR, W), BF),
            V((ZS, ZR, W), F32),
            V((ZS, ZR, W), BF),
            V((ZS, ZR, W), F32),
            V((2, YS, ZR, W), F32),
            V((ZS, ZR, W), BF),
            V((ZS, ZR, W), BF),
            V((ZS, ZR, W), F32),
            V((ZS, ZR, W), F32),
            V((MR, W), BF),
            V((MR, W), F32),
            dma((7,)),
            dma((4,)),
            dma((FIRST,)), dma((FIRST,)),
            dma((T,)), dma((T,)),
            dma((3, NX)), dma((3, NX)),
            dma((4,)), dma((4,)),
            dma((2,)), dma((2,)),
            dma((5, NX)), dma((5, NX)),
            dma((4,)), dma((4,)),
            dma((4, ZS)), dma((4, ZS)),
            dma((2, YS)), dma((2, YS)),
            dma((LATE, NX)), dma((LATE, NX)),
        ],
        compiler_params=pltpu.CompilerParams(
            collective_id=0, has_side_effects=True, vmem_limit_bytes=60 << 20
        ),
    )(
        send_order, enc_slot, enc_dest, proc_src, proc_dest, grid_in.T,
        w_embed, enc_coef.reshape(EP * W, W), mesh_in,
        proc_coef.reshape(PP * W, W), w_node, out_grad,
    )
    return pl.pallas_call(
        finish,
        out_shape=(
            jax.ShapeDtypeStruct((MR, W), BF),
            jax.ShapeDtypeStruct((MR, W), F32),
            jax.ShapeDtypeStruct((C_IN, W), F32),
            jax.ShapeDtypeStruct((LAT, W), F32),
        ),
        in_specs=[vmem] * 6,
        out_specs=(vmem,) * 4,
        compiler_params=pltpu.CompilerParams(vmem_limit_bytes=60 << 20),
    )(*parts)


def solution(mesh):
    return jax.shard_map(
        on_device,
        mesh=mesh,
        in_specs=(
            P("band", None),
            P(None, "chan"),
            P("band", None),
            P("band", None, None),
            P("band", None),
            P("band", None),
            P("band", "chan"),
            P("band", None, None),
            P("band", None),
            P("band", None),
            P(None, "chan"),
            P("band", "chan"),
        ),
        out_specs=(P("band", "chan"), P("band", "chan"), P(None, "chan"), P(None, "chan")),
        check_vma=False,
    )
```

```python
import jax
import jax.numpy as jnp
from jax import lax
from jax.experimental import pallas as pl
from jax.experimental.pallas import tpu as pltpu
from jax.sharding import PartitionSpec as P

MESH = pl.DeviceIdType.MESH
F32 = jnp.float32
BF = jnp.bfloat16
NB = 64
NX = 4
C_IN = 474
CP = 480
LAT = 512
W = 128
T = NB // NX
EP = 96
PP = 48
MB = 5
MR = MB * W
ER = T * W
CELLS = MB * T
LATE = 2
LATE_CELLS = MB * NX * LATE
OWN = 1
FIRST = 4
ZS = 8
YS = 4
ZR = 32
HALF = CP // 2


def place_of(t):
    return (3 * t + 13) & (T - 1)


def dot(a, b):
    return jnp.dot(a, b, preferred_element_type=F32)


def slope_of(v, s):
    return s * (1.0 + v * (1.0 - s))


def al(v, m):
    return pl.multiple_of(v, m)


def finish(out_in, grad_in, fin, fin2, node_fin, node_fin2, mesh_out, mesh_grad, gemb, gnode):
    core = lax.rem(lax.axis_index("band"), 2)
    mesh_out[...] = out_in[...]
    mesh_grad[...] = grad_in[...]
    gnode[pl.ds(al(core * 256, 256), 256), :] = node_fin[...].reshape(256, W)
    gnode[pl.ds(al((1 - core) * 256, 256), 256), :] = node_fin2[...].reshape(256, W)

    def write(low, high):
        gemb[0:HALF, :] = low[...].reshape(256, W)[:HALF].astype(F32)
        gemb[HALF:C_IN, :] = high[...].reshape(256, W)[: C_IN - HALF].astype(F32)

    @pl.when(core == 0)
    def _():
        write(fin, fin2)

    @pl.when(core == 1)
    def _():
        write(fin2, fin)


def kernel(
    order_in, eslot_in, edest_in, psrc_in, pdest_in, grid, wemb, ecoef, meshin, pcoef, wnode, ograd,
    mesh_out, mesh_grad, fin_out, fin2_out, node_out, node2_out,
    order, eslot, edest, psrc, pdest, flat, flat_last, blocks, stage, recv, we_all, wtmp, og_all, wn, wr_all, mi, ce,
    wide, cells, a_enc, a_late, a_proc, at_proc, gh, slope,
    part, enc_sum, enc_slope_f, rs1, lat_out, lat_in, ext, hid_all, hb_out, hb_in, mid, gn_out, gn_in, ge_all, gp,
    half_f, half_out, half_in, gemb_out, rs2, node_in, pieces_e, pieces_n, landed_e, landed_n, by_y, fin_e, fin_e2, fin_n, fin_n2, mo, mg,
    lsem, i_s, g_s, f_s, f_r, a_s, a_r, x_s, x_r, h_s, h_r, b_s, b_r, c_s, c_r, t_s, t_r, u_s, u_r, v_s, v_r, l_s, l_r,
):
    me = lax.axis_index("band")
    x = lax.axis_index("chan")
    core = lax.rem(me, 2)
    chip = lax.div(me, 2)
    mine = pl.ds(al(x * W, W), W)

    def to_band(src, dst, ss, rs, band):
        return pltpu.make_async_remote_copy(src, dst, ss, rs, device_id={"band": band}, device_id_type=MESH)

    def to_chan(src, dst, ss, rs, chan):
        return pltpu.make_async_remote_copy(src, dst, ss, rs, device_id={"chan": chan}, device_id_type=MESH)

    def peer(dx):
        return lax.rem(x + dx, NX)

    def cols(c):
        return pl.ds(al(c * W, W), W)

    def rows_of(c):
        return pl.ds(al(c * W, W), W)

    barrier = pltpu.get_barrier_semaphore()

    def greet(band):
        pl.semaphore_signal(barrier, inc=1, device_id={"band": band}, device_id_type=MESH)

    z_here = lax.div(me, 8)
    y_here = lax.rem(chip, YS)
    has_low = me > 0
    has_high = me < NB - 1
    low = lax.rem(me + NB - 1, NB)
    high = lax.rem(me + 1, NB)
    sibling = me + 1 - 2 * core

    def at_z(j):
        return lax.rem(me + 8 * j, NB)

    def at_y(j):
        return z_here * 8 + lax.rem(y_here + j, YS) * 2 + core

    def greet_source(t, _):
        @pl.when(x + t != 0)
        def _():
            greet(lax.rem(me - x - NX * t + 2 * NB, NB))

        return 0

    lax.fori_loop(0, T, greet_source, 0)
    pl.when(has_low)(lambda: greet(low))
    pl.when(has_high)(lambda: greet(high))
    greet(sibling)
    for j in range(1, ZS):
        greet(at_z(j))
    for j in range(1, YS):
        greet(at_y(j))
    for dx in range(1, NX):
        pl.semaphore_signal(barrier, inc=1, device_id={"chan": peer(dx)}, device_id_type=MESH)
    greetings = T + 2 + 1 + ZS - 1 + YS - 1 + NX - 1
    absent = jnp.where(x == 0, 1, 0) + jnp.where(me == 0, 1, 0) + jnp.where(me == NB - 1, 1, 0)

    ids = ((order_in, order), (eslot_in, eslot), (edest_in, edest), (psrc_in, psrc), (pdest_in, pdest))
    load_ids = [pltpu.make_async_copy(src, dst, i_s.at[i]) for i, (src, dst) in enumerate(ids)]
    load_ids[0].start()
    steps = ((0, 128), (128, 256), (256, 384), (384, C_IN))
    load_grid = [
        pltpu.make_async_copy(grid.at[a:b, :], flat_last if i == 3 else flat.at[i % 2], g_s.at[i])
        for i, (a, b) in enumerate(steps)
    ]
    for i in (0, 1, 3):
        load_grid[i].start()
    load_wemb = pltpu.make_async_copy(wemb, wtmp, lsem.at[1])
    load_og = pltpu.make_async_copy(ograd, og_all.at[:, mine], lsem.at[2])
    load_wn = pltpu.make_async_copy(wnode, wn, lsem.at[3])
    load_mi = pltpu.make_async_copy(meshin, mi, lsem.at[4])
    load_ce = pltpu.make_async_copy(ecoef, ce, lsem.at[5])
    cp = ce.at[0 : PP * W, :]
    load_cp = pltpu.make_async_copy(pcoef, cp, lsem.at[6])
    for c in load_ids[1:]:
        c.start()
    load_wemb.start()
    load_og.start()
    load_wn.start()

    stage[:, CP - 16 :, :] = jnp.zeros((T, 16, W), BF)
    def band_of(t):
        return lax.rem(me + x + NX * place_of(t), NB)

    def first_copy(t):
        rows = pl.ds(0, W)
        return to_band(stage.at[t, rows, :], recv.at[rows, cols(t)], f_s.at[t], f_r.at[t], band_of(t))

    def rest_copy(t):
        rows = pl.ds(W, CP - W)
        return to_band(stage.at[t, rows, :], recv.at[rows, cols(t)], a_s.at[t], a_r.at[t], band_of(t))

    def grid_copy(t):
        return to_band(stage.at[t], recv.at[:, cols(t)], a_s.at[t], a_r.at[t], band_of(t))

    def over_slots(lo, hi, body):
        def one(t, _):
            pl.when(x + place_of(t) != 0)(lambda: body(t))
            return 0

        lax.fori_loop(lo, hi, one, 0)

    for i, (a, b) in enumerate(steps):
        load_grid[i].wait()

        def by_block(k, _, i=i, n=b - a):
            blocks[k, 0:n, :] = flat_last[:, cols(k)] if i == 3 else flat[i % 2, :, cols(k)]
            return 0

        lax.fori_loop(0, NB, by_block, 0, unroll=4)
        if i == 0:
            load_grid[2].start()

        if i == 0:
            load_ids[0].wait()

        def to_stage(t, _, a=a, b=b):
            stage[t, a:b, :] = blocks[order[0, band_of(t)], 0 : b - a, :]
            return 0

        lax.fori_loop(0, T, to_stage, 0, unroll=2)
        if i == 0:
            pl.semaphore_wait(barrier, greetings - absent)
            over_slots(0, FIRST, lambda t: first_copy(t).start())
    over_slots(0, FIRST, lambda t: rest_copy(t).start())
    over_slots(FIRST, T - LATE, lambda t: grid_copy(t).start())
    load_mi.start()
    load_ce.start()

    @pl.when(x == 0)
    def _():
        recv[:, OWN * W : (OWN + 1) * W] = stage[OWN]

    load_wemb.wait()
    we_all[mine, CP - W : CP] = jnp.zeros((W, W), BF)
    we_all[mine, :C_IN] = wtmp[...].astype(F32).T.astype(BF)
    load_og.wait()
    load_wn.wait()
    wr_all[:, mine] = wn[mine, :]

    def early(dx):
        p = peer(dx)
        return (
            to_chan(we_all.at[mine, :], we_all.at[mine, :], x_s.at[0, dx], x_r.at[0, dx], p),
            to_chan(og_all.at[:, mine], og_all.at[:, mine], x_s.at[1, dx], x_r.at[1, dx], p),
            to_chan(wn.at[rows_of(p), :], wr_all.at[:, mine], x_s.at[2, dx], x_r.at[2, dx], p),
        )

    for dx in range(1, NX):
        for c in early(dx):
            c.start()

    def sum_cells(coef, pairs, count, hits):
        wide[0 : pairs * W, :] = coef[...].astype(F32)
        pick = jnp.where(hits, 1.0, 0.0).astype(BF)

        def one(i, _):
            line = wide[pl.ds(i, pairs, stride=W), :].astype(BF)
            cells[pl.ds(i, count, stride=W), :] = dot(pick, line)
            return 0

        lax.fori_loop(0, W, one, 0, unroll=4)

    def cell_ids(pairs):
        cell = lax.broadcasted_iota(jnp.int32, (CELLS, pairs), 0)
        return lax.shift_right_logical(cell, 4), lax.bitwise_and(cell, T - 1)

    for c in load_ids[1:]:
        c.wait()
    load_ce.wait()
    cell = lax.broadcasted_iota(jnp.int32, (CELLS + LATE_CELLS, EP), 0)
    tail = cell - CELLS
    own_group = cell < CELLS
    cell_m = jnp.where(own_group, lax.shift_right_logical(cell, 4), lax.shift_right_arithmetic(tail, 3))
    cell_t = jnp.where(own_group, lax.bitwise_and(cell, T - 1), T - LATE + lax.bitwise_and(tail, LATE - 1))
    cell_x = jnp.where(own_group, x, lax.bitwise_and(lax.shift_right_arithmetic(tail, 1), NX - 1))
    cell_slot = lax.bitwise_and(me - cell_x - NX * place_of(cell_t) + 2 * NB, NB - 1)
    sum_cells(ce, EP, CELLS + LATE_CELLS, (edest[...] == cell_m) & (eslot[...] == cell_slot))

    load_cp.start()

    def enc_cells(t, _):
        for m in range(MB):
            a_enc[m * W : (m + 1) * W, cols(t)] = cells[rows_of(m * T + t), :].astype(BF)
        return 0

    lax.fori_loop(0, T, enc_cells, 0)

    def late_cells(t, _):
        for m in range(MB):
            a_late[m * W : (m + 1) * W, cols(t)] = cells[rows_of(CELLS + m * NX * LATE + t), :].astype(BF)
        return 0

    lax.fori_loop(0, NX * LATE, late_cells, 0)

    load_cp.wait()
    cell_m, cell_s = cell_ids(PP)
    sum_cells(cp, PP, CELLS, (pdest[...] == cell_m) & (psrc[...] == cell_s))

    def proc_cells(s, _):
        for m in range(MB):
            block = cells[rows_of(m * T + s), :]
            a_proc[m * W : (m + 1) * W, cols(s)] = block.astype(BF)
            at_proc[rows_of(s), m * W : (m + 1) * W] = block.T.astype(BF)
        return 0

    lax.fori_loop(0, 3 * MB, proc_cells, 0)

    for dx in range(1, NX):
        for c in early(dx):
            c.wait_recv()
    gh[...] = lax.dot_general(og_all[...], wr_all[...], (((1,), (1,)), ((), ())), preferred_element_type=F32)

    def sent_first(t):
        first_copy(t).wait_send()
        rest_copy(t).wait_send()

    over_slots(0, FIRST, sent_first)
    over_slots(FIRST, 8, lambda t: grid_copy(t).wait_send())
    over_slots(T - LATE, T, lambda t: grid_copy(t).start())
    over_slots(8, T - LATE, lambda t: grid_copy(t).wait_send())

    def dot_nt(a, b):
        return lax.dot_general(a, b, (((1,), (1,)), ((), ())), preferred_element_type=F32)

    enc_sum[...] = jnp.zeros((MR, LAT), F32)

    def embed(here):
        pre = dot(we_all[...], recv[:, here])
        sig = jax.nn.sigmoid(pre)
        slope[:, here] = slope_of(pre, sig)
        return (pre * sig).astype(BF)

    def embed_sum(u, _):
        here = pl.ds(al(u * 2 * W, 2 * W), 2 * W)
        latent = embed(here)
        enc_sum[...] += dot_nt(a_enc[:, here], latent)
        return 0

    def first_slots(u, _):
        def arrive(t):
            first_copy(t).wait_recv()
            rest_copy(t).wait_recv()

        over_slots(2 * u, 2 * u + 2, arrive)
        return embed_sum(u, 0)

    def other_slots(u, _):
        over_slots(2 * u, 2 * u + 2, lambda t: grid_copy(t).wait_recv())
        return embed_sum(u, 0)

    lax.fori_loop(0, FIRST // 2, first_slots, 0)
    lax.fori_loop(FIRST // 2, (T - LATE) // 2, other_slots, 0)

    half = lax.div(x, 2)
    away = 1 - half
    twin = x + 1 - 2 * lax.rem(x, 2)
    far = (2 * away, 2 * away + 1)

    def two(h):
        return pl.ds(al(h * 2 * W, 2 * W), 2 * W)

    def enc_copy(c):
        return to_chan(part.at[:, cols(c)], rs1.at[x], c_s.at[0, c], c_r.at[0, x], c)

    part[:, two(away)] = enc_sum[:, two(away)].astype(BF)
    for c in far:
        enc_copy(c).start()
    part[:, cols(twin)] = enc_sum[:, cols(twin)].astype(BF)
    enc_copy(twin).start()

    def late_copy(v, c):
        return to_chan(lat_out.at[v, rows_of(c), :], lat_in.at[x, v], l_s.at[v, c], l_r.at[v, x], c)

    for v in range(LATE):
        t = T - LATE + v
        grid_copy(t).wait_recv()
        lat_out[v] = embed(pl.ds(t * W, W))
        for c in (*far, twin):
            late_copy(v, c).start()
    load_mi.wait()

    def late_sum(c):
        out = jnp.zeros((MR, W), F32)
        for v in range(LATE):
            out = out + dot_nt(a_late[:, cols(c * LATE + v)], lat_in[c, v])
        return out

    lat_in[x] = lat_out[:, mine, :]
    enc_pre = enc_sum[:, mine] + late_sum(x)
    for dx in range(1, NX):
        p = peer(dx)
        to_chan(part.at[:, cols(p)], rs1.at[p], c_s.at[0, p], c_r.at[0, p], p).wait_recv()
        enc_pre = enc_pre + rs1[p].astype(F32)
    for c in (twin, *far):
        for v in range(LATE):
            to_chan(lat_out.at[v, rows_of(c), :], lat_in.at[c, v], l_s.at[v, c], l_r.at[v, c], c).wait_recv()
        enc_pre = enc_pre + late_sum(c)
    enc_sig = jax.nn.sigmoid(enc_pre)
    mesh_one = (mi[...].astype(F32) + enc_pre * enc_sig).astype(BF)
    enc_slope = slope_of(enc_pre, enc_sig)
    enc_slope_f[...] = enc_slope

    ext[MR : 2 * MR, :] = mesh_one
    own_ext = ext.at[MR : 2 * MR, :]
    halo_up = to_band(own_ext, ext.at[0:MR, :], h_s.at[0], h_r.at[0], high)
    halo_down = to_band(own_ext, ext.at[2 * MR : 3 * MR, :], h_s.at[1], h_r.at[1], low)
    pl.when(has_high)(halo_up.start)
    pl.when(has_low)(halo_down.start)
    mid[...] = dot(a_proc[:, MR : 2 * MR], mesh_one)

    @pl.when(me == 0)
    def _():
        ext[0:MR, :] = jnp.zeros((MR, W), BF)

    @pl.when(me == NB - 1)
    def _():
        ext[2 * MR : 3 * MR, :] = jnp.zeros((MR, W), BF)

    pl.when(has_low)(halo_up.wait_recv)
    mid[...] += dot(a_proc[:, 0:MR], ext[0:MR, :])
    pl.when(has_high)(halo_down.wait_recv)
    proc_pre = mid[...] + dot(a_proc[:, 2 * MR : 3 * MR], ext[2 * MR : 3 * MR, :])
    proc_sig = jax.nn.sigmoid(proc_pre)
    hidden = (proc_pre * proc_sig).astype(BF)
    hid_all[:, mine] = hidden

    def hid_copy(c):
        return to_chan(hid_all.at[:, mine], hid_all.at[:, mine], c_s.at[1, c], c_r.at[1, x], c)

    grad_proc = (gh[...] * slope_of(proc_pre, proc_sig)).astype(BF)

    hb_out[0] = dot(at_proc[0:MR, :], grad_proc).astype(BF)
    back_down = to_band(hb_out.at[0], hb_in.at[0], b_s.at[0], b_r.at[0], low)
    pl.when(has_low)(back_down.start)
    hb_out[1] = dot(at_proc[2 * MR : 3 * MR, :], grad_proc).astype(BF)
    back_up = to_band(hb_out.at[1], hb_in.at[1], b_s.at[1], b_r.at[1], high)
    pl.when(has_high)(back_up.start)
    mid[...] = dot(at_proc[MR : 2 * MR, :], grad_proc) + og_all[:, mine].astype(F32)

    gn_out[...] = dot(hidden.astype(F32).T.astype(BF), og_all[...])
    gn_in[mine, :] = gn_out[:, mine]

    def gn_copy(c):
        return to_chan(gn_out.at[:, cols(c)], gn_in.at[mine, :], c_s.at[2, c], c_r.at[2, x], c)

    for dx in range(1, NX):
        gn_copy(peer(dx)).start()

    @pl.when(me == NB - 1)
    def _():
        hb_in[0] = jnp.zeros((MR, W), BF)

    @pl.when(me == 0)
    def _():
        hb_in[1] = jnp.zeros((MR, W), BF)

    pl.when(has_high)(back_down.wait_recv)
    pl.when(has_low)(back_up.wait_recv)
    total = mid[...] + hb_in[0].astype(F32) + hb_in[1].astype(F32)
    mg[...] = total
    save_grad = pltpu.make_async_copy(mg, mesh_grad, lsem.at[1])
    save_grad.start()
    ge_all[mine, :] = (total * enc_slope_f[...]).T.astype(BF)

    def ge_copy(c):
        return to_chan(ge_all.at[mine, :], ge_all.at[mine, :], c_s.at[3, c], c_r.at[3, x], c)

    def ge_wait(c):
        to_chan(ge_all.at[rows_of(c), :], ge_all.at[rows_of(c), :], c_s.at[3, c], c_r.at[3, c], c).wait_recv()

    for c in (twin, *far):
        ge_copy(c).start()

    keep = pl.ds(al(core * 256, 256), 256)
    give = pl.ds(al((1 - core) * 256, 256), 256)
    pieces = (pieces_e, pieces_n)
    landed = (landed_e, landed_n)
    result = (fin_e, fin_n)
    other = (fin_e2, fin_n2)

    def z_of(j):
        return lax.rem(z_here + j, ZS)

    def sum_z(k, j):
        return to_band(pieces[k].at[z_of(j)], landed[k].at[z_here], u_s.at[k, j], u_r.at[k, j], at_z(j))

    def sum_y(k, j):
        return to_band(by_y.at[k, y_here], by_y.at[k, y_here], v_s.at[k, j], v_r.at[k, j], at_y(j))

    def back_z(k, j):
        return to_band(result[k].at[z_here], result[k].at[z_here], u_s.at[2 + k, j], u_r.at[2 + k, j], at_z(j))

    def start_z(k):
        for j in range(1, ZS):
            sum_z(k, j).start()
        landed[k][z_here] = pieces[k][z_here]

    def start_y(k):
        for j in range(1, ZS):
            sum_z(k, j).wait_recv()
        by_y[k, y_here] = jnp.sum(landed[k][...].astype(F32), axis=0)
        for j in range(1, YS):
            sum_y(k, j).start()

    def start_back(k):
        for j in range(1, YS):
            y = lax.rem(y_here - j + YS, YS)
            to_band(by_y.at[k, y], by_y.at[k, y], v_s.at[k, j], v_r.at[k, j], at_y(j)).wait_recv()
        result[k][z_here] = jnp.sum(by_y[k], axis=0).astype(result[k].dtype)
        for j in range(1, ZS):
            back_z(k, j).start()

    def swap_back(k):
        for j in range(1, ZS):
            z = lax.rem(z_here - j + ZS, ZS)
            to_band(result[k].at[z], result[k].at[z], u_s.at[2 + k, j], u_r.at[2 + k, j], at_z(j)).wait_recv()
        copy = to_band(result[k], other[k], t_s.at[2 + k], t_r.at[2 + k], sibling)
        copy.start()
        return copy

    for dx in range(1, NX):
        p = peer(dx)
        prow = pl.ds(al(p * W, W), W)
        to_chan(gn_out.at[:, cols(p)], gn_in.at[prow, :], c_s.at[2, p], c_r.at[2, p], p).wait_recv()
    node_swap = to_band(gn_in.at[give, :], node_in, t_s.at[0], t_r.at[0], sibling)
    node_swap.start()
    node_swap.wait_recv()
    pieces_n[...] = (gn_in[keep, :] + node_in[...]).reshape(ZS, ZR, W)
    start_z(1)

    gemb_f = enc_sum.at[0:CP, 0 : 2 * W]

    def back(h):
        def piece(t, _):
            here = pl.ds(al(t * 512, 512), 512)
            msg = dot(ge_all[two(h), :], a_enc[:, here])
            gp[:, here] = (msg * slope[two(h), here]).astype(BF)
            return 0

        lax.fori_loop(0, ER // 512, piece, 0)
        gemb_f[...] = dot_nt(recv[...], gp[...])

    keep_rows = pl.ds(al(core * HALF, 16), HALF)
    give_rows = pl.ds(al((1 - core) * HALF, 16), HALF)

    def half_copy(k):
        return to_band(half_out.at[k], half_in.at[k], h_s.at[2 + k], h_r.at[2 + k], sibling)

    def ge2_copy(c):
        return to_chan(gemb_out.at[:, cols(c)], rs2.at[x], c_s.at[4, c], c_r.at[4, x], c)

    ge_wait(twin)
    back(half)
    half_out[0] = gemb_f[give_rows, :]
    half_copy(0).start()
    half_f[0] = gemb_f[keep_rows, :]
    start_y(1)
    for c in far:
        ge_wait(c)
    back(away)
    half_out[1] = gemb_f[give_rows, :]
    half_copy(1).start()
    half_f[1] = gemb_f[keep_rows, :]
    half_copy(0).wait_recv()
    half_f[0] = half_f[0] + half_in[0]
    gemb_out[:, two(half)] = half_f[0].astype(BF)
    ge2_copy(twin).start()
    half_copy(1).wait_recv()
    gemb_out[:, two(away)] = (half_f[1] + half_in[1]).astype(BF)
    for c in far:
        ge2_copy(c).start()
    start_back(1)
    total = half_f[0, :, pl.ds(al(lax.rem(x, 2) * W, W), W)]
    for dx in range(1, NX):
        p = peer(dx)
        to_chan(gemb_out.at[:, cols(p)], rs2.at[p], c_s.at[4, p], c_r.at[4, p], p).wait_recv()
        total = total + rs2[p].astype(F32)
    padded = jnp.concatenate([total, jnp.zeros((ZS * ZR - HALF, W), F32)], axis=0)
    pieces_e[...] = padded.astype(BF).reshape(ZS, ZR, W)
    start_z(0)
    for dx in range(1, NX):
        hid_copy(peer(dx)).start()
    node_back = swap_back(1)
    start_y(0)
    start_back(0)

    for dx in range(1, NX):
        p = peer(dx)
        to_chan(hid_all.at[:, cols(p)], hid_all.at[:, cols(p)], c_s.at[1, p], c_r.at[1, p], p).wait_recv()
    mo[...] = (ext[MR : 2 * MR, :].astype(F32) + dot(hid_all[...], wn[...])).astype(BF)
    save_out = pltpu.make_async_copy(mo, mesh_out, lsem.at[2])
    save_out.start()
    node_back.wait_recv()
    node_saves = [pltpu.make_async_copy(fin_n, node_out, lsem.at[3]), pltpu.make_async_copy(fin_n2, node2_out, lsem.at[4])]
    for c in node_saves:
        c.start()
    last_back = swap_back(0)
    last_save = pltpu.make_async_copy(fin_e, fin_out, lsem.at[5])
    last_save.start()
    last_back.wait_recv()
    last_save2 = pltpu.make_async_copy(fin_e2, fin2_out, lsem.at[6])
    last_save2.start()
    saves = (*node_saves, last_save, last_save2)

    over_slots(T - LATE, T, lambda t: grid_copy(t).wait_send())
    for dx in range(1, NX):
        p = peer(dx)
        for c in early(dx):
            c.wait_send()
        for v in range(LATE):
            late_copy(v, p).wait_send()
        for f in (enc_copy, hid_copy, gn_copy, ge_copy, ge2_copy):
            f(p).wait_send()
    pl.when(has_high)(halo_up.wait_send)
    pl.when(has_low)(halo_down.wait_send)
    pl.when(has_low)(back_down.wait_send)
    pl.when(has_high)(back_up.wait_send)
    for k in range(2):
        half_copy(k).wait_send()
    for c in (node_swap, node_back, last_back):
        c.wait_send()

    for k in range(2):
        for j in range(1, ZS):
            sum_z(k, j).wait_send()
            back_z(k, j).wait_send()
        for j in range(1, YS):
            sum_y(k, j).wait_send()
    save_grad.wait()
    save_out.wait()
    for c in saves:
        c.wait()


def on_device(
    grid_in, w_embed, send_order, enc_coef, enc_slot, enc_dest, mesh_in, proc_coef, proc_src, proc_dest, w_node, out_grad
):
    hbm = pl.BlockSpec(memory_space=pl.ANY)
    vmem = pl.BlockSpec(memory_space=pltpu.VMEM)
    V = pltpu.VMEM
    dma = pltpu.SemaphoreType.DMA
    piece = jax.ShapeDtypeStruct((ZS, ZR, W), F32)
    piece_bf = jax.ShapeDtypeStruct((ZS, ZR, W), BF)
    parts = pl.pallas_call(
        kernel,
        out_shape=(
            jax.ShapeDtypeStruct((MR, W), BF),
            jax.ShapeDtypeStruct((MR, W), F32),
            piece_bf, piece_bf, piece, piece,
        ),
        in_specs=[hbm] * 12,
        out_specs=(hbm,) * 6,
        scratch_shapes=[
            pltpu.SMEM((1, NB), jnp.int32),
            V((1, EP), jnp.int32),
            V((1, EP), jnp.int32),
            V((1, PP), jnp.int32),
            V((1, PP), jnp.int32),
            V((2, W, NB * W), BF),
            V((C_IN - 3 * W, NB * W), BF),
            V((NB, W, W), BF),
            V((T, CP, W), BF),
            V((CP, ER), BF),
            V((LAT, CP), BF),
            V((C_IN, W), BF),
            V((MR, LAT), BF),
            V((LAT, W), BF),
            V((W, LAT), BF),
            V((MR, W), BF),
            V((EP * W, W), BF),
            V((EP * W, W), F32),
            V(((CELLS + LATE_CELLS) * W, W), F32),
            V((MR, ER), BF),
            V((MR, NX * LATE * W), BF),
            V((MR, 3 * MR), BF),
            V((3 * MR, MR), BF),
            V((MR, W), F32),
            V((LAT, ER), F32),
            V((MR, LAT), BF),
            V((MR, LAT), F32),
            V((MR, W), F32),
            V((NX, MR, W), BF),
            V((LATE, LAT, W), BF),
            V((NX, LATE, W, W), BF),
            V((3 * MR, W), BF),
            V((MR, LAT), BF),
            V((2, MR, W), BF),
            V((2, MR, W), BF),
            V((MR, W), F32),
            V((W, LAT), F32),
            V((LAT, W), F32),
            V((LAT, MR), BF),
            V((2 * W, ER), BF),
            V((2, HALF, 2 * W), F32),
            V((2, HALF, 2 * W), F32),
            V((2, HALF, 2 * W), F32),
            V((HALF, LAT), BF),
            V((NX, HALF, W), BF),
            V((256, W), F32),
            V((ZS, ZR, W), BF),
            V((ZS, ZR, W), F32),
            V((ZS, ZR, W), BF),
            V((ZS, ZR, W), F32),
            V((2, YS, ZR, W), F32),
            V((ZS, ZR, W), BF),
            V((ZS, ZR, W), BF),
            V((ZS, ZR, W), F32),
            V((ZS, ZR, W), F32),
            V((MR, W), BF),
            V((MR, W), F32),
            dma((7,)),
            dma((5,)),
            dma((4,)),
            dma((FIRST,)), dma((FIRST,)),
            dma((T,)), dma((T,)),
            dma((3, NX)), dma((3, NX)),
            dma((4,)), dma((4,)),
            dma((2,)), dma((2,)),
            dma((5, NX)), dma((5, NX)),
            dma((4,)), dma((4,)),
            dma((4, ZS)), dma((4, ZS)),
            dma((2, YS)), dma((2, YS)),
            dma((LATE, NX)), dma((LATE, NX)),
        ],
        compiler_params=pltpu.CompilerParams(
            collective_id=0, has_side_effects=True, vmem_limit_bytes=60 << 20
        ),
    )(
        send_order, enc_slot, enc_dest, proc_src, proc_dest, grid_in.T,
        w_embed, enc_coef.reshape(EP * W, W), mesh_in,
        proc_coef.reshape(PP * W, W), w_node, out_grad,
    )
    return pl.pallas_call(
        finish,
        out_shape=(
            jax.ShapeDtypeStruct((MR, W), BF),
            jax.ShapeDtypeStruct((MR, W), F32),
            jax.ShapeDtypeStruct((C_IN, W), F32),
            jax.ShapeDtypeStruct((LAT, W), F32),
        ),
        in_specs=[vmem] * 6,
        out_specs=(vmem,) * 4,
        compiler_params=pltpu.CompilerParams(vmem_limit_bytes=60 << 20),
    )(*parts)


def solution(mesh):
    return jax.shard_map(
        on_device,
        mesh=mesh,
        in_specs=(
            P("band", None),
            P(None, "chan"),
            P("band", None),
            P("band", None, None),
            P("band", None),
            P("band", None),
            P("band", "chan"),
            P("band", None, None),
            P("band", None),
            P("band", None),
            P(None, "chan"),
            P("band", "chan"),
        ),
        out_specs=(P("band", "chan"), P("band", "chan"), P(None, "chan"), P(None, "chan")),
        check_vma=False,
    )
```

```python
import jax
import jax.numpy as jnp
from jax import lax
from jax.experimental import pallas as pl
from jax.experimental.pallas import tpu as pltpu
from jax.sharding import PartitionSpec as P

MESH = pl.DeviceIdType.MESH
F32 = jnp.float32
BF = jnp.bfloat16
NB = 64
NX = 4
C_IN = 474
CP = 480
LAT = 512
W = 128
T = NB // NX
EP = 96
PP = 48
MB = 5
MR = MB * W
ER = T * W
CELLS = MB * T
LATE = 2
LATE_CELLS = MB * NX * LATE
OWN = 1
FIRST = 4
ZS = 8
YS = 4
ZR = 32
HALF = CP // 2


def place_of(t):
    return (3 * t + 13) & (T - 1)


def dot(a, b):
    return jnp.dot(a, b, preferred_element_type=F32)


def slope_of(v, s):
    return s * (1.0 + v * (1.0 - s))


def al(v, m):
    return pl.multiple_of(v, m)


def finish(out_in, grad_in, fin, fin2, node_fin, node_fin2, mesh_out, mesh_grad, gemb, gnode):
    core = lax.rem(lax.axis_index("band"), 2)
    mesh_out[...] = out_in[...]
    mesh_grad[...] = grad_in[...]
    gnode[pl.ds(al(core * 256, 256), 256), :] = node_fin[...].reshape(256, W)
    gnode[pl.ds(al((1 - core) * 256, 256), 256), :] = node_fin2[...].reshape(256, W)

    def write(low, high):
        gemb[0:HALF, :] = low[...].reshape(256, W)[:HALF].astype(F32)
        gemb[HALF:C_IN, :] = high[...].reshape(256, W)[: C_IN - HALF].astype(F32)

    @pl.when(core == 0)
    def _():
        write(fin, fin2)

    @pl.when(core == 1)
    def _():
        write(fin2, fin)


def kernel(
    order_in, eslot_in, edest_in, psrc_in, pdest_in, grid, wemb, ecoef, meshin, pcoef, wnode, ograd,
    mesh_out, mesh_grad, fin_out, fin2_out, node_out, node2_out,
    order, eslot, edest, psrc, pdest, flat, flat_last, blocks, stage, recv, we_all, wtmp, og_all, wn, wr_all, mi, ce,
    wide, cells, a_enc, a_late, a_proc, at_proc, gh, slope,
    part, enc_sum, enc_slope_f, rs1, lat_out, lat_in, ext, hid_all, hb_out, hb_in, mid, gn_out, gn_in, ge_all, gp,
    half_f, half_out, half_in, gemb_out, rs2, node_in, pieces_e, pieces_n, landed_e, landed_n, by_y, fin_e, fin_e2, fin_n, fin_n2, mo, mg,
    lsem, i_s, g_s, f_s, f_r, a_s, a_r, x_s, x_r, h_s, h_r, b_s, b_r, c_s, c_r, t_s, t_r, u_s, u_r, v_s, v_r, l_s, l_r,
):
    me = lax.axis_index("band")
    x = lax.axis_index("chan")
    core = lax.rem(me, 2)
    chip = lax.div(me, 2)
    mine = pl.ds(al(x * W, W), W)

    def to_band(src, dst, ss, rs, band):
        return pltpu.make_async_remote_copy(src, dst, ss, rs, device_id={"band": band}, device_id_type=MESH)

    def to_chan(src, dst, ss, rs, chan):
        return pltpu.make_async_remote_copy(src, dst, ss, rs, device_id={"chan": chan}, device_id_type=MESH)

    def peer(dx):
        return lax.rem(x + dx, NX)

    def cols(c):
        return pl.ds(al(c * W, W), W)

    def rows_of(c):
        return pl.ds(al(c * W, W), W)

    steps = ((0, 128), (128, 256), (256, 384), (384, C_IN))
    load_grid = [
        pltpu.make_async_copy(grid.at[a:b, :], flat_last if i == 3 else flat.at[i % 2], g_s.at[i])
        for i, (a, b) in enumerate(steps)
    ]
    load_grid[0].start()

    barrier = pltpu.get_barrier_semaphore()

    def greet(band):
        pl.semaphore_signal(barrier, inc=1, device_id={"band": band}, device_id_type=MESH)

    z_here = lax.div(me, 8)
    y_here = lax.rem(chip, YS)
    has_low = me > 0
    has_high = me < NB - 1
    low = lax.rem(me + NB - 1, NB)
    high = lax.rem(me + 1, NB)
    sibling = me + 1 - 2 * core

    def at_z(j):
        return lax.rem(me + 8 * j, NB)

    def at_y(j):
        return z_here * 8 + lax.rem(y_here + j, YS) * 2 + core

    def greet_source(t, _):
        @pl.when(x + t != 0)
        def _():
            greet(lax.rem(me - x - NX * t + 2 * NB, NB))

        return 0

    lax.fori_loop(0, T, greet_source, 0)
    pl.when(has_low)(lambda: greet(low))
    pl.when(has_high)(lambda: greet(high))
    greet(sibling)
    for j in range(1, ZS):
        greet(at_z(j))
    for j in range(1, YS):
        greet(at_y(j))
    for dx in range(1, NX):
        pl.semaphore_signal(barrier, inc=1, device_id={"chan": peer(dx)}, device_id_type=MESH)
    greetings = T + 2 + 1 + ZS - 1 + YS - 1 + NX - 1
    absent = jnp.where(x == 0, 1, 0) + jnp.where(me == 0, 1, 0) + jnp.where(me == NB - 1, 1, 0)

    ids = ((order_in, order), (eslot_in, eslot), (edest_in, edest), (psrc_in, psrc), (pdest_in, pdest))
    load_ids = [pltpu.make_async_copy(src, dst, i_s.at[i]) for i, (src, dst) in enumerate(ids)]
    load_ids[0].start()
    for i in (1, 3):
        load_grid[i].start()
    load_wemb = pltpu.make_async_copy(wemb, wtmp, lsem.at[1])
    load_og = pltpu.make_async_copy(ograd, og_all.at[:, mine], lsem.at[2])
    load_wn = pltpu.make_async_copy(wnode, wn, lsem.at[3])
    load_mi = pltpu.make_async_copy(meshin, mi, lsem.at[4])
    load_ce = pltpu.make_async_copy(ecoef, ce, lsem.at[5])
    cp = ce.at[0 : PP * W, :]
    load_cp = pltpu.make_async_copy(pcoef, cp, lsem.at[6])
    for c in load_ids[1:]:
        c.start()
    load_wemb.start()
    load_og.start()
    load_wn.start()

    stage[:, CP - 16 :, :] = jnp.zeros((T, 16, W), BF)
    def band_of(t):
        return lax.rem(me + x + NX * place_of(t), NB)

    def first_copy(t):
        rows = pl.ds(0, W)
        return to_band(stage.at[t, rows, :], recv.at[rows, cols(t)], f_s.at[t], f_r.at[t], band_of(t))

    def rest_copy(t):
        rows = pl.ds(W, CP - W)
        return to_band(stage.at[t, rows, :], recv.at[rows, cols(t)], a_s.at[t], a_r.at[t], band_of(t))

    def grid_copy(t):
        return to_band(stage.at[t], recv.at[:, cols(t)], a_s.at[t], a_r.at[t], band_of(t))

    def over_slots(lo, hi, body):
        def one(t, _):
            pl.when(x + place_of(t) != 0)(lambda: body(t))
            return 0

        lax.fori_loop(lo, hi, one, 0)

    for i, (a, b) in enumerate(steps):
        load_grid[i].wait()

        def by_block(k, _, i=i, n=b - a):
            blocks[k, 0:n, :] = flat_last[:, cols(k)] if i == 3 else flat[i % 2, :, cols(k)]
            return 0

        lax.fori_loop(0, NB, by_block, 0, unroll=4)
        if i == 0:
            load_grid[2].start()

        if i == 0:
            load_ids[0].wait()

        def to_stage(t, _, a=a, b=b):
            stage[t, a:b, :] = blocks[order[0, band_of(t)], 0 : b - a, :]
            return 0

        lax.fori_loop(0, T, to_stage, 0, unroll=2)
        if i == 0:
            pl.semaphore_wait(barrier, greetings - absent)
            over_slots(0, FIRST, lambda t: first_copy(t).start())
    over_slots(0, FIRST, lambda t: rest_copy(t).start())
    over_slots(FIRST, T - LATE, lambda t: grid_copy(t).start())
    load_mi.start()
    load_ce.start()

    @pl.when(x == 0)
    def _():
        recv[:, OWN * W : (OWN + 1) * W] = stage[OWN]

    load_wemb.wait()
    we_all[mine, CP - W : CP] = jnp.zeros((W, W), BF)
    we_all[mine, :C_IN] = wtmp[...].astype(F32).T.astype(BF)
    load_og.wait()
    load_wn.wait()
    wr_all[:, mine] = wn[mine, :]

    def early(dx):
        p = peer(dx)
        return (
            to_chan(we_all.at[mine, :], we_all.at[mine, :], x_s.at[0, dx], x_r.at[0, dx], p),
            to_chan(og_all.at[:, mine], og_all.at[:, mine], x_s.at[1, dx], x_r.at[1, dx], p),
            to_chan(wn.at[rows_of(p), :], wr_all.at[:, mine], x_s.at[2, dx], x_r.at[2, dx], p),
        )

    for dx in range(1, NX):
        for c in early(dx):
            c.start()

    def sum_cells(coef, pairs, count, hits):
        wide[0 : pairs * W, :] = coef[...].astype(F32)
        pick = jnp.where(hits, 1.0, 0.0).astype(BF)

        def one(i, _):
            line = wide[pl.ds(i, pairs, stride=W), :].astype(BF)
            cells[pl.ds(i, count, stride=W), :] = dot(pick, line)
            return 0

        lax.fori_loop(0, W, one, 0, unroll=4)

    def cell_ids(pairs):
        cell = lax.broadcasted_iota(jnp.int32, (CELLS, pairs), 0)
        return lax.shift_right_logical(cell, 4), lax.bitwise_and(cell, T - 1)

    for c in load_ids[1:]:
        c.wait()
    load_ce.wait()
    cell = lax.broadcasted_iota(jnp.int32, (CELLS + LATE_CELLS, EP), 0)
    tail = cell - CELLS
    own_group = cell < CELLS
    cell_m = jnp.where(own_group, lax.shift_right_logical(cell, 4), lax.shift_right_arithmetic(tail, 3))
    cell_t = jnp.where(own_group, lax.bitwise_and(cell, T - 1), T - LATE + lax.bitwise_and(tail, LATE - 1))
    cell_x = jnp.where(own_group, x, lax.bitwise_and(lax.shift_right_arithmetic(tail, 1), NX - 1))
    cell_slot = lax.bitwise_and(me - cell_x - NX * place_of(cell_t) + 2 * NB, NB - 1)
    sum_cells(ce, EP, CELLS + LATE_CELLS, (edest[...] == cell_m) & (eslot[...] == cell_slot))

    load_cp.start()

    def enc_cells(t, _):
        for m in range(MB):
            a_enc[m * W : (m + 1) * W, cols(t)] = cells[rows_of(m * T + t), :].astype(BF)
        return 0

    lax.fori_loop(0, T, enc_cells, 0)

    def late_cells(t, _):
        for m in range(MB):
            a_late[m * W : (m + 1) * W, cols(t)] = cells[rows_of(CELLS + m * NX * LATE + t), :].astype(BF)
        return 0

    lax.fori_loop(0, NX * LATE, late_cells, 0)

    load_cp.wait()
    cell_m, cell_s = cell_ids(PP)
    sum_cells(cp, PP, CELLS, (pdest[...] == cell_m) & (psrc[...] == cell_s))

    def proc_cells(s, _):
        for m in range(MB):
            block = cells[rows_of(m * T + s), :]
            a_proc[m * W : (m + 1) * W, cols(s)] = block.astype(BF)
            at_proc[rows_of(s), m * W : (m + 1) * W] = block.T.astype(BF)
        return 0

    lax.fori_loop(0, 3 * MB, proc_cells, 0)

    for dx in range(1, NX):
        for c in early(dx):
            c.wait_recv()
    gh[...] = lax.dot_general(og_all[...], wr_all[...], (((1,), (1,)), ((), ())), preferred_element_type=F32)

    def sent_first(t):
        first_copy(t).wait_send()
        rest_copy(t).wait_send()

    over_slots(0, FIRST, sent_first)
    over_slots(FIRST, 8, lambda t: grid_copy(t).wait_send())
    over_slots(T - LATE, T, lambda t: grid_copy(t).start())
    over_slots(8, T - LATE, lambda t: grid_copy(t).wait_send())

    def dot_nt(a, b):
        return lax.dot_general(a, b, (((1,), (1,)), ((), ())), preferred_element_type=F32)

    enc_sum[...] = jnp.zeros((MR, LAT), F32)

    def embed(here):
        pre = dot(we_all[...], recv[:, here])
        sig = jax.nn.sigmoid(pre)
        slope[:, here] = slope_of(pre, sig)
        return (pre * sig).astype(BF)

    def embed_sum(u, _):
        here = pl.ds(al(u * 2 * W, 2 * W), 2 * W)
        latent = embed(here)
        enc_sum[...] += dot_nt(a_enc[:, here], latent)
        return 0

    def first_slots(u, _):
        def arrive(t):
            first_copy(t).wait_recv()
            rest_copy(t).wait_recv()

        over_slots(2 * u, 2 * u + 2, arrive)
        return embed_sum(u, 0)

    def other_slots(u, _):
        over_slots(2 * u, 2 * u + 2, lambda t: grid_copy(t).wait_recv())
        return embed_sum(u, 0)

    lax.fori_loop(0, FIRST // 2, first_slots, 0)
    lax.fori_loop(FIRST // 2, (T - LATE) // 2, other_slots, 0)

    half = lax.div(x, 2)
    away = 1 - half
    twin = x + 1 - 2 * lax.rem(x, 2)
    far = (2 * away, 2 * away + 1)

    def two(h):
        return pl.ds(al(h * 2 * W, 2 * W), 2 * W)

    def enc_copy(c):
        return to_chan(part.at[:, cols(c)], rs1.at[x], c_s.at[0, c], c_r.at[0, x], c)

    part[:, two(away)] = enc_sum[:, two(away)].astype(BF)
    for c in far:
        enc_copy(c).start()
    part[:, cols(twin)] = enc_sum[:, cols(twin)].astype(BF)
    enc_copy(twin).start()

    def late_copy(v, c):
        return to_chan(lat_out.at[v, rows_of(c), :], lat_in.at[x, v], l_s.at[v, c], l_r.at[v, x], c)

    for v in range(LATE):
        t = T - LATE + v
        grid_copy(t).wait_recv()
        lat_out[v] = embed(pl.ds(t * W, W))
        for c in (*far, twin):
            late_copy(v, c).start()
    load_mi.wait()

    def late_sum(c):
        out = jnp.zeros((MR, W), F32)
        for v in range(LATE):
            out = out + dot_nt(a_late[:, cols(c * LATE + v)], lat_in[c, v])
        return out

    lat_in[x] = lat_out[:, mine, :]
    enc_pre = enc_sum[:, mine] + late_sum(x)
    for dx in range(1, NX):
        p = peer(dx)
        to_chan(part.at[:, cols(p)], rs1.at[p], c_s.at[0, p], c_r.at[0, p], p).wait_recv()
        enc_pre = enc_pre + rs1[p].astype(F32)
    for c in (twin, *far):
        for v in range(LATE):
            to_chan(lat_out.at[v, rows_of(c), :], lat_in.at[c, v], l_s.at[v, c], l_r.at[v, c], c).wait_recv()
        enc_pre = enc_pre + late_sum(c)
    enc_sig = jax.nn.sigmoid(enc_pre)
    mesh_one = (mi[...].astype(F32) + enc_pre * enc_sig).astype(BF)
    enc_slope = slope_of(enc_pre, enc_sig)
    enc_slope_f[...] = enc_slope

    ext[MR : 2 * MR, :] = mesh_one
    own_ext = ext.at[MR : 2 * MR, :]
    halo_up = to_band(own_ext, ext.at[0:MR, :], h_s.at[0], h_r.at[0], high)
    halo_down = to_band(own_ext, ext.at[2 * MR : 3 * MR, :], h_s.at[1], h_r.at[1], low)
    pl.when(has_high)(halo_up.start)
    pl.when(has_low)(halo_down.start)
    mid[...] = dot(a_proc[:, MR : 2 * MR], mesh_one)

    @pl.when(me == 0)
    def _():
        ext[0:MR, :] = jnp.zeros((MR, W), BF)

    @pl.when(me == NB - 1)
    def _():
        ext[2 * MR : 3 * MR, :] = jnp.zeros((MR, W), BF)

    pl.when(has_low)(halo_up.wait_recv)
    mid[...] += dot(a_proc[:, 0:MR], ext[0:MR, :])
    pl.when(has_high)(halo_down.wait_recv)
    proc_pre = mid[...] + dot(a_proc[:, 2 * MR : 3 * MR], ext[2 * MR : 3 * MR, :])
    proc_sig = jax.nn.sigmoid(proc_pre)
    hidden = (proc_pre * proc_sig).astype(BF)
    hid_all[:, mine] = hidden

    def hid_copy(c):
        return to_chan(hid_all.at[:, mine], hid_all.at[:, mine], c_s.at[1, c], c_r.at[1, x], c)

    grad_proc = (gh[...] * slope_of(proc_pre, proc_sig)).astype(BF)

    hb_out[0] = dot(at_proc[0:MR, :], grad_proc).astype(BF)
    back_down = to_band(hb_out.at[0], hb_in.at[0], b_s.at[0], b_r.at[0], low)
    pl.when(has_low)(back_down.start)
    hb_out[1] = dot(at_proc[2 * MR : 3 * MR, :], grad_proc).astype(BF)
    back_up = to_band(hb_out.at[1], hb_in.at[1], b_s.at[1], b_r.at[1], high)
    pl.when(has_high)(back_up.start)
    mid[...] = dot(at_proc[MR : 2 * MR, :], grad_proc) + og_all[:, mine].astype(F32)

    gn_out[...] = dot(hidden.astype(F32).T.astype(BF), og_all[...])
    gn_in[mine, :] = gn_out[:, mine]

    def gn_copy(c):
        return to_chan(gn_out.at[:, cols(c)], gn_in.at[mine, :], c_s.at[2, c], c_r.at[2, x], c)

    for dx in range(1, NX):
        gn_copy(peer(dx)).start()

    @pl.when(me == NB - 1)
    def _():
        hb_in[0] = jnp.zeros((MR, W), BF)

    @pl.when(me == 0)
    def _():
        hb_in[1] = jnp.zeros((MR, W), BF)

    pl.when(has_high)(back_down.wait_recv)
    pl.when(has_low)(back_up.wait_recv)
    total = mid[...] + hb_in[0].astype(F32) + hb_in[1].astype(F32)
    mg[...] = total
    save_grad = pltpu.make_async_copy(mg, mesh_grad, lsem.at[1])
    save_grad.start()
    ge_all[mine, :] = (total * enc_slope_f[...]).T.astype(BF)

    def ge_copy(c):
        return to_chan(ge_all.at[mine, :], ge_all.at[mine, :], c_s.at[3, c], c_r.at[3, x], c)

    def ge_wait(c):
        to_chan(ge_all.at[rows_of(c), :], ge_all.at[rows_of(c), :], c_s.at[3, c], c_r.at[3, c], c).wait_recv()

    for c in (twin, *far):
        ge_copy(c).start()

    keep = pl.ds(al(core * 256, 256), 256)
    give = pl.ds(al((1 - core) * 256, 256), 256)
    pieces = (pieces_e, pieces_n)
    landed = (landed_e, landed_n)
    result = (fin_e, fin_n)
    other = (fin_e2, fin_n2)

    def z_of(j):
        return lax.rem(z_here + j, ZS)

    def sum_z(k, j):
        return to_band(pieces[k].at[z_of(j)], landed[k].at[z_here], u_s.at[k, j], u_r.at[k, j], at_z(j))

    def sum_y(k, j):
        return to_band(by_y.at[k, y_here], by_y.at[k, y_here], v_s.at[k, j], v_r.at[k, j], at_y(j))

    def back_z(k, j):
        return to_band(result[k].at[z_here], result[k].at[z_here], u_s.at[2 + k, j], u_r.at[2 + k, j], at_z(j))

    def start_z(k):
        for j in range(1, ZS):
            sum_z(k, j).start()
        landed[k][z_here] = pieces[k][z_here]

    def start_y(k):
        for j in range(1, ZS):
            sum_z(k, j).wait_recv()
        by_y[k, y_here] = jnp.sum(landed[k][...].astype(F32), axis=0)
        for j in range(1, YS):
            sum_y(k, j).start()

    def start_back(k):
        for j in range(1, YS):
            y = lax.rem(y_here - j + YS, YS)
            to_band(by_y.at[k, y], by_y.at[k, y], v_s.at[k, j], v_r.at[k, j], at_y(j)).wait_recv()
        result[k][z_here] = jnp.sum(by_y[k], axis=0).astype(result[k].dtype)
        for j in range(1, ZS):
            back_z(k, j).start()

    def swap_back(k):
        for j in range(1, ZS):
            z = lax.rem(z_here - j + ZS, ZS)
            to_band(result[k].at[z], result[k].at[z], u_s.at[2 + k, j], u_r.at[2 + k, j], at_z(j)).wait_recv()
        copy = to_band(result[k], other[k], t_s.at[2 + k], t_r.at[2 + k], sibling)
        copy.start()
        return copy

    for dx in range(1, NX):
        p = peer(dx)
        prow = pl.ds(al(p * W, W), W)
        to_chan(gn_out.at[:, cols(p)], gn_in.at[prow, :], c_s.at[2, p], c_r.at[2, p], p).wait_recv()
    node_swap = to_band(gn_in.at[give, :], node_in, t_s.at[0], t_r.at[0], sibling)
    node_swap.start()
    node_swap.wait_recv()
    pieces_n[...] = (gn_in[keep, :] + node_in[...]).reshape(ZS, ZR, W)
    start_z(1)

    gemb_f = enc_sum.at[0:CP, 0 : 2 * W]

    def back(h):
        def piece(t, _):
            here = pl.ds(al(t * 512, 512), 512)
            msg = dot(ge_all[two(h), :], a_enc[:, here])
            gp[:, here] = (msg * slope[two(h), here]).astype(BF)
            return 0

        lax.fori_loop(0, ER // 512, piece, 0)
        gemb_f[...] = dot_nt(recv[...], gp[...])

    keep_rows = pl.ds(al(core * HALF, 16), HALF)
    give_rows = pl.ds(al((1 - core) * HALF, 16), HALF)

    def half_copy(k):
        return to_band(half_out.at[k], half_in.at[k], h_s.at[2 + k], h_r.at[2 + k], sibling)

    def ge2_copy(c):
        return to_chan(gemb_out.at[:, cols(c)], rs2.at[x], c_s.at[4, c], c_r.at[4, x], c)

    ge_wait(twin)
    back(half)
    half_out[0] = gemb_f[give_rows, :]
    half_copy(0).start()
    half_f[0] = gemb_f[keep_rows, :]
    start_y(1)
    for c in far:
        ge_wait(c)
    back(away)
    half_out[1] = gemb_f[give_rows, :]
    half_copy(1).start()
    half_f[1] = gemb_f[keep_rows, :]
    half_copy(0).wait_recv()
    half_f[0] = half_f[0] + half_in[0]
    gemb_out[:, two(half)] = half_f[0].astype(BF)
    ge2_copy(twin).start()
    half_copy(1).wait_recv()
    gemb_out[:, two(away)] = (half_f[1] + half_in[1]).astype(BF)
    for c in far:
        ge2_copy(c).start()
    start_back(1)
    total = half_f[0, :, pl.ds(al(lax.rem(x, 2) * W, W), W)]
    for dx in range(1, NX):
        p = peer(dx)
        to_chan(gemb_out.at[:, cols(p)], rs2.at[p], c_s.at[4, p], c_r.at[4, p], p).wait_recv()
        total = total + rs2[p].astype(F32)
    padded = jnp.concatenate([total, jnp.zeros((ZS * ZR - HALF, W), F32)], axis=0)
    pieces_e[...] = padded.astype(BF).reshape(ZS, ZR, W)
    start_z(0)
    for dx in range(1, NX):
        hid_copy(peer(dx)).start()
    node_back = swap_back(1)
    start_y(0)
    start_back(0)

    for dx in range(1, NX):
        p = peer(dx)
        to_chan(hid_all.at[:, cols(p)], hid_all.at[:, cols(p)], c_s.at[1, p], c_r.at[1, p], p).wait_recv()
    mo[...] = (ext[MR : 2 * MR, :].astype(F32) + dot(hid_all[...], wn[...])).astype(BF)
    save_out = pltpu.make_async_copy(mo, mesh_out, lsem.at[2])
    save_out.start()
    node_back.wait_recv()
    node_saves = [pltpu.make_async_copy(fin_n, node_out, lsem.at[3]), pltpu.make_async_copy(fin_n2, node2_out, lsem.at[4])]
    for c in node_saves:
        c.start()
    last_back = swap_back(0)
    last_save = pltpu.make_async_copy(fin_e, fin_out, lsem.at[5])
    last_save.start()
    last_back.wait_recv()
    last_save2 = pltpu.make_async_copy(fin_e2, fin2_out, lsem.at[6])
    last_save2.start()
    saves = (*node_saves, last_save, last_save2)

    over_slots(T - LATE, T, lambda t: grid_copy(t).wait_send())
    for dx in range(1, NX):
        p = peer(dx)
        for c in early(dx):
            c.wait_send()
        for v in range(LATE):
            late_copy(v, p).wait_send()
        for f in (enc_copy, hid_copy, gn_copy, ge_copy, ge2_copy):
            f(p).wait_send()
    pl.when(has_high)(halo_up.wait_send)
    pl.when(has_low)(halo_down.wait_send)
    pl.when(has_low)(back_down.wait_send)
    pl.when(has_high)(back_up.wait_send)
    for k in range(2):
        half_copy(k).wait_send()
    for c in (node_swap, node_back, last_back):
        c.wait_send()

    for k in range(2):
        for j in range(1, ZS):
            sum_z(k, j).wait_send()
            back_z(k, j).wait_send()
        for j in range(1, YS):
            sum_y(k, j).wait_send()
    save_grad.wait()
    save_out.wait()
    for c in saves:
        c.wait()


def on_device(
    grid_in, w_embed, send_order, enc_coef, enc_slot, enc_dest, mesh_in, proc_coef, proc_src, proc_dest, w_node, out_grad
):
    hbm = pl.BlockSpec(memory_space=pl.ANY)
    vmem = pl.BlockSpec(memory_space=pltpu.VMEM)
    V = pltpu.VMEM
    dma = pltpu.SemaphoreType.DMA
    piece = jax.ShapeDtypeStruct((ZS, ZR, W), F32)
    piece_bf = jax.ShapeDtypeStruct((ZS, ZR, W), BF)
    parts = pl.pallas_call(
        kernel,
        out_shape=(
            jax.ShapeDtypeStruct((MR, W), BF),
            jax.ShapeDtypeStruct((MR, W), F32),
            piece_bf, piece_bf, piece, piece,
        ),
        in_specs=[hbm] * 12,
        out_specs=(hbm,) * 6,
        scratch_shapes=[
            pltpu.SMEM((1, NB), jnp.int32),
            V((1, EP), jnp.int32),
            V((1, EP), jnp.int32),
            V((1, PP), jnp.int32),
            V((1, PP), jnp.int32),
            V((2, W, NB * W), BF),
            V((C_IN - 3 * W, NB * W), BF),
            V((NB, W, W), BF),
            V((T, CP, W), BF),
            V((CP, ER), BF),
            V((LAT, CP), BF),
            V((C_IN, W), BF),
            V((MR, LAT), BF),
            V((LAT, W), BF),
            V((W, LAT), BF),
            V((MR, W), BF),
            V((EP * W, W), BF),
            V((EP * W, W), F32),
            V(((CELLS + LATE_CELLS) * W, W), F32),
            V((MR, ER), BF),
            V((MR, NX * LATE * W), BF),
            V((MR, 3 * MR), BF),
            V((3 * MR, MR), BF),
            V((MR, W), F32),
            V((LAT, ER), F32),
            V((MR, LAT), BF),
            V((MR, LAT), F32),
            V((MR, W), F32),
            V((NX, MR, W), BF),
            V((LATE, LAT, W), BF),
            V((NX, LATE, W, W), BF),
            V((3 * MR, W), BF),
            V((MR, LAT), BF),
            V((2, MR, W), BF),
            V((2, MR, W), BF),
            V((MR, W), F32),
            V((W, LAT), F32),
            V((LAT, W), F32),
            V((LAT, MR), BF),
            V((2 * W, ER), BF),
            V((2, HALF, 2 * W), F32),
            V((2, HALF, 2 * W), F32),
            V((2, HALF, 2 * W), F32),
            V((HALF, LAT), BF),
            V((NX, HALF, W), BF),
            V((256, W), F32),
            V((ZS, ZR, W), BF),
            V((ZS, ZR, W), F32),
            V((ZS, ZR, W), BF),
            V((ZS, ZR, W), F32),
            V((2, YS, ZR, W), F32),
            V((ZS, ZR, W), BF),
            V((ZS, ZR, W), BF),
            V((ZS, ZR, W), F32),
            V((ZS, ZR, W), F32),
            V((MR, W), BF),
            V((MR, W), F32),
            dma((7,)),
            dma((5,)),
            dma((4,)),
            dma((FIRST,)), dma((FIRST,)),
            dma((T,)), dma((T,)),
            dma((3, NX)), dma((3, NX)),
            dma((4,)), dma((4,)),
            dma((2,)), dma((2,)),
            dma((5, NX)), dma((5, NX)),
            dma((4,)), dma((4,)),
            dma((4, ZS)), dma((4, ZS)),
            dma((2, YS)), dma((2, YS)),
            dma((LATE, NX)), dma((LATE, NX)),
        ],
        compiler_params=pltpu.CompilerParams(
            collective_id=0, has_side_effects=True, vmem_limit_bytes=60 << 20
        ),
    )(
        send_order, enc_slot, enc_dest, proc_src, proc_dest, grid_in.T,
        w_embed, enc_coef.reshape(EP * W, W), mesh_in,
        proc_coef.reshape(PP * W, W), w_node, out_grad,
    )
    return pl.pallas_call(
        finish,
        out_shape=(
            jax.ShapeDtypeStruct((MR, W), BF),
            jax.ShapeDtypeStruct((MR, W), F32),
            jax.ShapeDtypeStruct((C_IN, W), F32),
            jax.ShapeDtypeStruct((LAT, W), F32),
        ),
        in_specs=[vmem] * 6,
        out_specs=(vmem,) * 4,
        compiler_params=pltpu.CompilerParams(vmem_limit_bytes=60 << 20),
    )(*parts)


def solution(mesh):
    return jax.shard_map(
        on_device,
        mesh=mesh,
        in_specs=(
            P("band", None),
            P(None, "chan"),
            P("band", None),
            P("band", None, None),
            P("band", None),
            P("band", None),
            P("band", "chan"),
            P("band", None, None),
            P("band", None),
            P("band", None),
            P(None, "chan"),
            P("band", "chan"),
        ),
        out_specs=(P("band", "chan"), P("band", "chan"), P(None, "chan"), P(None, "chan")),
        check_vma=False,
    )
```
